128 devices in a mesh: sub: 16 (over x_lo, z, core), blk: 8 (over x_hi, y).
Axes of the slice: x: 4 (x_hi: 2, x_lo: 2; x = x_hi * 2 + x_lo), y: 4, z: 4, core: 2. Of those that a mesh axis runs over, the one named last changes fastest.
Arguments:
- residual: bfloat16 [16, 4096, 3072], P('sub', 'blk')
- lower_factor: bfloat16 [16, 3072, 3072], P('sub', 'blk'), as said below
- upper_factor: bfloat16 [16, 3072, 3072], P('sub', 'blk')
- margin_rows: int32 [16, 2, 512], P('sub'), may hold values from 0 to 3071, as said below
- blend: float32 [16, 2, 512], P('sub'), may hold values from 0.2 to 0.8
Outputs:
- basis: bfloat16 [16, 4096, 3072], P('sub', 'blk')
- gram: float32 [4096, 512], P('blk')
The draws below stay inside these ranges and needn't reach their ends.
Inputs may be any that keep to these rules, and one draw needn't show every extreme that they name: `margin_rows`: within one subdomain all 1024 entries are distinct, and 0 and 3071 occur in every subdomain. Entry k of the second half of subdomain s and entry k of the first half of subdomain s + 1 name the same shared unknown. lower_factor is zero above the diagonal and upper_factor below it; both diagonals are positive.
All inputs are finite; a program needn't handle non-finite values.
Results may differ from the reference program's by a relative error of at most 0.019.
Values may be sent and summed in bfloat16 or wider, within the bound.
A program may use at most 128 MiB of HBM per device.

```python
import math
import jax
import jax.numpy as jnp
from jax import lax

UNKNOWNS = 3072
SHOT_BLOCK = 512
MARGIN = 512
SUBDOMAINS = 16
SHOTS = 4096


def triangle(key, sign, spread, diag_lo, diag_hi):
    key_off, key_diag = jax.random.split(key)
    off = jax.random.normal(key_off, (SUBDOMAINS, UNKNOWNS, UNKNOWNS), jnp.float32) * (spread / math.sqrt(UNKNOWNS))
    diag = jnp.exp(jax.random.uniform(key_diag, (SUBDOMAINS, UNKNOWNS), jnp.float32, math.log(diag_lo), math.log(diag_hi)))
    rows = jax.lax.broadcasted_iota(jnp.int32, (UNKNOWNS, UNKNOWNS), 0)
    cols = jax.lax.broadcasted_iota(jnp.int32, (UNKNOWNS, UNKNOWNS), 1)
    keep = (cols - rows) * sign > 0
    diagonal_mask = rows == cols
    shaped = jnp.where(keep[None], off, jnp.float32(0.0))
    return jnp.where(diagonal_mask[None], diag[:, :, None], shaped)


def draw_lower_factor(key, part):
    key = jax.random.fold_in(key, 11)
    return triangle(key, -1, 1.0, 0.5, 2.0).astype(jnp.bfloat16)


def draw_upper_factor(key, part):
    key = jax.random.fold_in(key, 23)
    return triangle(key, 1, 1.0, 0.5, 2.0).astype(jnp.bfloat16)


def scaled_field(key, noise, rise):
    key_shot, key_row = jax.random.split(key)
    shot_scale = jnp.exp(jax.random.uniform(key_shot, (SUBDOMAINS, SHOTS, 1), jnp.float32, 0.0, math.log(10.0)))
    row_scale = jnp.exp(jax.random.uniform(key_row, (SUBDOMAINS, 1, UNKNOWNS), jnp.float32, 0.0, math.log(10.0)))
    where = jax.lax.broadcasted_iota(jnp.float32, (SUBDOMAINS, 1, 1), 0) / max(SUBDOMAINS - 1, 1)
    return noise * shot_scale * row_scale * jnp.sqrt(1.0 + rise * where) * 0.1


def draw_residual(key, part):
    key = jax.random.fold_in(key, 37)
    key_noise, key_rest = jax.random.split(key)
    noise = jax.random.normal(key_noise, (SUBDOMAINS, SHOTS, UNKNOWNS), jnp.float32)
    return scaled_field(key_rest, noise, 2.0).astype(jnp.bfloat16)


def draw_margin_rows(key, part):
    key = jax.random.fold_in(key, 53)
    keys = jax.random.split(key, SUBDOMAINS)

    def single(sub_key):
        key_rest, key_order = jax.random.split(sub_key)
        others = 1 + jax.random.permutation(key_rest, UNKNOWNS - 2).astype(jnp.int32)
        ends = jnp.array([0, UNKNOWNS - 1], jnp.int32)
        chosen = jnp.concatenate([ends, others[:2 * MARGIN - 2]])
        order = jax.random.permutation(key_order, 2 * MARGIN)
        return chosen[order].reshape(2, MARGIN)
    return jax.vmap(single)(keys)


def steps_of(stream_key, extent, cuts, smallest, high):
    gain, own = 1.0, jax.random.fold_in(stream_key, 6)
    for axis_at, parts in cuts:
        draws = jnp.exp(jax.random.uniform(jax.random.fold_in(own, axis_at), (parts,), jnp.float32, smallest / len(cuts), high / len(cuts)))
        gain = gain * jnp.repeat(draws, extent[axis_at] // parts).reshape([-1 if axis == axis_at else 1 for axis in range(len(extent))])
    return gain


def setup_inputs(seed: int = 0) -> dict:
    seeds = jax.random.split(jax.random.key(seed), 6)
    residual = draw_residual(jax.random.fold_in(seeds[5], 71), 0)
    lower_factor = draw_lower_factor(jax.random.fold_in(seeds[5], 71), 0)
    upper_factor = draw_upper_factor(jax.random.fold_in(seeds[5], 71), 0)
    margin_rows = draw_margin_rows(jax.random.fold_in(seeds[5], 71), 0)
    blend = jnp.clip(0.2 + 0.6 * jax.random.uniform(seeds[4], (SUBDOMAINS, 2, MARGIN), jnp.float32) ** steps_of(seeds[4], (SUBDOMAINS, 2, MARGIN), ((0, 16),), -0.2, 0.2), 0.2, 0.8)
    return {"residual": residual, "lower_factor": lower_factor, "upper_factor": upper_factor, "margin_rows": margin_rows, "blend": blend}


def solve_one(operands):
    rhs, lower, upper = operands
    interim = jnp.dot(rhs, lower.T, preferred_element_type=jnp.float32).astype(jnp.bfloat16)
    return jnp.dot(interim, upper.T, preferred_element_type=jnp.float32).astype(jnp.bfloat16)

def pick_columns(values, rows):
    return values[:, rows]

def put_columns(values, rows, fresh):
    return values.at[:, rows].set(fresh)

def reference(residual, lower_factor, upper_factor, margin_rows, blend):
    local = lax.map(solve_one, (residual, lower_factor, upper_factor))
    left_rows = margin_rows[:, 0, :]
    right_rows = margin_rows[:, 1, :]
    at_left = jax.vmap(pick_columns)(local, left_rows).astype(jnp.float32)
    at_right = jax.vmap(pick_columns)(local, right_rows).astype(jnp.float32)
    empty = jnp.zeros_like(at_left[:1])
    from_left = jnp.concatenate([empty, at_right[:-1]], axis=0)
    from_right = jnp.concatenate([at_left[1:], empty], axis=0)
    places = jnp.arange(SUBDOMAINS)
    has_left = (places > 0).astype(jnp.float32)[:, None, None]
    has_right = (places < SUBDOMAINS - 1).astype(jnp.float32)[:, None, None]
    new_left = at_left + blend[:, 0, :][:, None, :] * (from_left - at_left) * has_left
    new_right = at_right + blend[:, 1, :][:, None, :] * (from_right - at_right) * has_right
    widened = local.astype(jnp.float32)
    widened = jax.vmap(put_columns)(widened, left_rows, new_left)
    widened = jax.vmap(put_columns)(widened, right_rows, new_right)
    blended = widened.astype(jnp.bfloat16)
    wide = blended.astype(jnp.float32)
    squares = lax.optimization_barrier(jnp.sum(wide * wide, axis=(0, 2)))
    scale = 1.0 / jnp.sqrt(squares / (SUBDOMAINS * UNKNOWNS) + 1e-05)
    basis = (wide * scale[None, :, None]).astype(jnp.bfloat16)
    nblocks = SHOTS // SHOT_BLOCK
    wide_blocks = wide.reshape(SUBDOMAINS, nblocks, SHOT_BLOCK, UNKNOWNS)
    rhs_blocks = residual.astype(jnp.float32).reshape(SUBDOMAINS, nblocks, SHOT_BLOCK, UNKNOWNS)
    raw = jnp.einsum('sbiu,sbju->bij', wide_blocks, rhs_blocks)
    gram = raw * scale.reshape(nblocks, SHOT_BLOCK)[:, :, None] / (SUBDOMAINS * UNKNOWNS)
    return (basis, gram.reshape(SHOTS, SHOT_BLOCK))
```

```python
import jax
import jax.numpy as jnp
from jax import lax
from jax.experimental import pallas as pl
from jax.experimental.pallas import tpu as pltpu
from jax.sharding import PartitionSpec as P

MESH = pl.DeviceIdType.MESH
UNKNOWNS = 3072
SHOTS = 512
BLOCK = 384
HALF = BLOCK // 2
BLOCKS = UNKNOWNS // BLOCK
RINGS = 4
PIECES = 4
PIECE = SHOTS // PIECES


def times_rows(left, right):
    return lax.dot_general(
        left, right, (((1,), (1,)), ((), ())), preferred_element_type=jnp.float32
    )


def columns(k):
    return pl.ds(pl.multiple_of(k * BLOCK, BLOCK), BLOCK)


def solve_kernel(
    rhs_in,
    lower_in,
    upper_in,
    out,
    rhs,
    lower,
    upper,
    interim,
    local,
    own_sem,
    x_recv,
    x_send,
    r_recv,
    r_send,
    near_recv,
    near_send,
    far_recv,
    far_send,
    sib_recv,
    sib_send,
    ret_recv,
    ret_send,
    out_sem,
):
    sub = lax.axis_index("sub")
    blk = lax.axis_index("blk")
    core = sub % 2
    pair = sub - core
    half = blk // RINGS
    y = blk % RINGS
    guest = core != half
    home = core == half
    partner = (pair + 1 - core, (1 - half) * RINGS + y)
    sibling = (pair + 1 - core, blk)
    up = (sub, half * RINGS + (y + 1) % RINGS)
    down = (sub, half * RINGS + (y + 3) % RINGS)
    mine = core * RINGS + y
    below = core * RINGS + (y + 3) % RINGS
    above = core * RINGS + (y + 1) % RINGS
    across = core * RINGS + (y + 2) % RINGS

    barrier = pltpu.get_barrier_semaphore()
    for other in (partner, sibling, up, down):
        pl.semaphore_signal(barrier, inc=1, device_id=other, device_id_type=MESH)
    pl.semaphore_wait(barrier, 4)

    sources = (lower_in, upper_in)
    holds = (lower, upper)

    def span(w, b):
        return (0, b + 1) if w == 0 else (b, BLOCKS)

    def remote(src, dst, send, recv, device):
        return pltpu.make_async_remote_copy(
            src_ref=src,
            dst_ref=dst,
            send_sem=send,
            recv_sem=recv,
            device_id=device,
            device_id_type=MESH,
        )

    def whole(w, b, k):
        return holds[w].at[b, :, columns(k)]

    def part(w, b, k, top):
        return holds[w].at[b, pl.ds(0 if top else HALF, HALF), columns(k)]

    def exchange(w, k):
        return remote(
            sources[w].at[0, :, columns(k)],
            whole(w, blk, k),
            x_send.at[w, k],
            x_recv.at[w, k],
            partner,
        )

    def exchange_rhs(i):
        rows = pl.ds(i * PIECE, PIECE)
        return remote(rhs_in.at[0, rows], rhs.at[rows], r_send.at[i], r_recv.at[i], partner)

    def to_near(w, k, upward, src):
        d = 0 if upward else 1
        return remote(
            src,
            whole(w, mine, k),
            near_send.at[w, d, k],
            near_recv.at[w, d, k],
            up if upward else down,
        )

    def to_far(w, b, k, upward):
        d = 0 if upward else 1
        return remote(
            part(w, b, k, upward),
            part(w, b, k, upward),
            far_send.at[w, d, k],
            far_recv.at[w, d, k],
            up if upward else down,
        )

    def to_sibling(w, b, slot, k, src):
        return remote(
            src,
            whole(w, b, k),
            sib_send.at[w, slot, k],
            sib_recv.at[w, slot, k],
            sibling,
        )

    def each(w, b, step):
        first, last = span(w, b)

        def go(k, carry):
            step(k)
            return carry

        lax.fori_loop(first, last, go, 0)

    def send_own(w, src):
        def step(k):
            to_near(w, k, True, src(k)).start()
            to_near(w, k, False, src(k)).start()
            to_sibling(w, mine, 0, k, src(k)).start()

        return step

    def own_from_input(w):
        each(w, mine, send_own(w, lambda k: sources[w].at[0, :, columns(k)]))

    def own_from_partner(w):
        send = send_own(w, lambda k: whole(w, mine, k))

        def step(k):
            remote(
                whole(w, mine, k), whole(w, mine, k), x_send.at[w, k], x_recv.at[w, k], partner
            ).wait_recv()
            send(k)

        each(w, mine, step)

    def relay_from(w, upward, k):
        b = below if upward else above
        d = 0 if upward else 1
        remote(
            whole(w, b, k),
            whole(w, b, k),
            near_send.at[w, d, k],
            near_recv.at[w, d, k],
            up if upward else down,
        ).wait_recv()
        to_far(w, b, k, upward).start()
        to_sibling(w, b, 1 + d, k, whole(w, b, k)).start()

    def relay(w, j):
        for upward, b in ((True, below), (False, above)):
            first, last = span(w, b)

            @pl.when(first + j < last)
            def _():
                relay_from(w, upward, first + j)

    def relay_all(w):
        def go(j, carry):
            relay(w, j)
            return carry

        lax.fori_loop(0, BLOCKS, go, 0)

    def relay_across(w):
        def step(k):
            for upward in (True, False):
                to_far(w, across, k, upward).wait_recv()
            to_sibling(w, across, 3, k, whole(w, across, k)).start()

        each(w, across, step)

    def own_copy(w):
        return pltpu.make_async_copy(sources[w].at[0], holds[w].at[mine], own_sem.at[w])

    def rhs_copy():
        return pltpu.make_async_copy(rhs_in.at[0], rhs, own_sem.at[2])

    def turn(t):
        i = t % RINGS
        return jnp.where(i == 0, 0, jnp.where(i == 1, 3, i - 1))

    def from_sibling(w, slot):
        b = (1 - core) * RINGS + (y + turn(slot)) % RINGS

        def step(k):
            to_sibling(w, b, slot, k, whole(w, b, k)).wait_recv()

        each(w, b, step)

    @pl.when(home)
    def _():
        own_from_input(0)
        rhs_copy().start()
        own_copy(0).start()
        own_copy(1).start()
        relay_all(0)
        own_from_input(1)
        relay_across(0)
        relay_all(1)
        relay_across(1)
        rhs_copy().wait()
        own_copy(0).wait()
        own_copy(1).wait()

    @pl.when(guest)
    def _():
        each(0, blk, lambda k: exchange(0, k).start())
        own_from_partner(0)
        for i in range(PIECES):
            exchange_rhs(i).start()
        relay_all(0)
        relay_across(0)
        each(1, blk, lambda k: exchange(1, k).start())
        for i in range(PIECES):
            exchange_rhs(i).wait_recv()

    def wait_lower(slot, carry):
        from_sibling(0, slot)
        return carry

    lax.fori_loop(0, RINGS, wait_lower, 0)

    for b in range(BLOCKS):
        stop = (b + 1) * BLOCK
        interim[:, b * BLOCK : stop] = times_rows(rhs[:, :stop], lower[b, :, :stop]).astype(
            jnp.bfloat16
        )

    @pl.when(guest)
    def _():
        own_from_partner(1)

    def back(b):
        return remote(
            local.at[:, columns(b)],
            out.at[:, columns(b)],
            ret_send.at[b],
            ret_recv.at[b],
            partner,
        )

    def keep(b):
        return pltpu.make_async_copy(
            local.at[:, columns(b)], out.at[:, columns(b)], out_sem.at[b]
        )

    def solve_step(t, carry):
        ring = jnp.where(t < RINGS, half, 1 - half)

        @pl.when(guest & (t < RINGS))
        def _():
            relay(1, 2 * t)
            relay(1, 2 * t + 1)

        @pl.when(guest & (t == 2 * RINGS - 1))
        def _():
            relay_across(1)

        @pl.when(ring != core)
        def _():
            from_sibling(1, t % RINGS)

        block = ring * RINGS + (y + turn(t)) % RINGS
        for b in range(BLOCKS):

            @pl.when(block == b)
            def _():
                start = b * BLOCK
                local[:, start : start + BLOCK] = times_rows(
                    interim[:, start:], upper[b, :, start:]
                ).astype(jnp.bfloat16)

        @pl.when(guest)
        def _():
            back(block).start()

        @pl.when(home)
        def _():
            keep(block).start()

        return carry

    lax.fori_loop(0, BLOCKS, solve_step, 0)

    for w in range(2):

        def own_sent(k):
            to_near(w, k, True, whole(w, mine, k)).wait_send()
            to_near(w, k, False, whole(w, mine, k)).wait_send()
            to_sibling(w, mine, 0, k, whole(w, mine, k)).wait_send()

        each(w, mine, own_sent)
        for upward, b in ((True, below), (False, above)):
            slot = 1 if upward else 2

            def near_sent(k):
                to_far(w, b, k, upward).wait_send()
                to_sibling(w, b, slot, k, whole(w, b, k)).wait_send()

            each(w, b, near_sent)
        each(w, across, lambda k: to_sibling(w, across, 3, k, whole(w, across, k)).wait_send())

        @pl.when(guest)
        def _():
            each(w, blk, lambda k: exchange(w, k).wait_send())

    @pl.when(guest)
    def _():
        for i in range(PIECES):
            exchange_rhs(i).wait_send()

    def finish(b, carry):
        @pl.when(guest)
        def _():
            back(b).wait()

        @pl.when(home)
        def _():
            keep(b).wait()

        return carry

    lax.fori_loop(0, BLOCKS, finish, 0)


def solve(residual, lower_factor, upper_factor):
    dma = pltpu.SemaphoreType.DMA
    hbm = pl.BlockSpec(memory_space=pl.ANY)
    return pl.pallas_call(
        solve_kernel,
        out_shape=jax.ShapeDtypeStruct((SHOTS, UNKNOWNS), jnp.bfloat16),
        in_specs=[hbm] * 3,
        out_specs=hbm,
        scratch_shapes=[
            pltpu.VMEM((SHOTS, UNKNOWNS), jnp.bfloat16),
            pltpu.VMEM((BLOCKS, BLOCK, UNKNOWNS), jnp.bfloat16),
            pltpu.VMEM((BLOCKS, BLOCK, UNKNOWNS), jnp.bfloat16),
            pltpu.VMEM((SHOTS, UNKNOWNS), jnp.bfloat16),
            pltpu.VMEM((SHOTS, UNKNOWNS), jnp.bfloat16),
            dma((3,)),
            dma((2, BLOCKS)),
            dma((2, BLOCKS)),
            dma((PIECES,)),
            dma((PIECES,)),
            dma((2, 2, BLOCKS)),
            dma((2, 2, BLOCKS)),
            dma((2, 2, BLOCKS)),
            dma((2, 2, BLOCKS)),
            dma((2, RINGS, BLOCKS)),
            dma((2, RINGS, BLOCKS)),
            dma((BLOCKS,)),
            dma((BLOCKS,)),
            dma((BLOCKS,)),
        ],
        compiler_params=pltpu.CompilerParams(
            collective_id=0, has_side_effects=True, vmem_limit_bytes=60 * 1024 * 1024
        ),
        cost_estimate=pl.CostEstimate(
            flops=2 * 36 * 2 * SHOTS * BLOCK * BLOCK,
            bytes_accessed=5 * SHOTS * UNKNOWNS * 2,
            transcendentals=0,
        ),
    )(residual, lower_factor, upper_factor)


def shifted(block, axis, distance):
    devices = range(lax.axis_size(axis))
    route = [(i - distance, i) for i in devices if i - distance in devices]
    return lax.ppermute(block, axis, route)


def body(residual, lower_factor, upper_factor, margin_rows, blend):
    rhs = residual[0]
    local = solve(residual, lower_factor, upper_factor)
    left_rows = margin_rows[0, 0]
    right_rows = margin_rows[0, 1]
    at_left = local[:, left_rows]
    at_right = local[:, right_rows]
    from_left = shifted(at_right, "sub", 1).astype(jnp.float32)
    from_right = shifted(at_left, "sub", -1).astype(jnp.float32)
    position = lax.axis_index("sub")
    count = lax.axis_size("sub")
    has_left = (position > 0).astype(jnp.float32)
    has_right = (position < count - 1).astype(jnp.float32)
    left_value = at_left.astype(jnp.float32)
    right_value = at_right.astype(jnp.float32)
    new_left = left_value + blend[0, 0][None, :] * (from_left - left_value) * has_left
    new_right = right_value + blend[0, 1][None, :] * (from_right - right_value) * has_right
    widened = (
        local.astype(jnp.float32).at[:, left_rows].set(new_left).at[:, right_rows].set(new_right)
    )
    blended = widened.astype(jnp.bfloat16)
    wide = blended.astype(jnp.float32)
    partial_squares = jnp.sum(wide * wide, axis=1)
    raw = times_rows(blended, rhs)
    total_cells = count * local.shape[1]
    squares = lax.psum(partial_squares, "sub")
    scale = 1.0 / jnp.sqrt(squares / total_cells + 1e-05)
    gram = lax.psum((raw * (scale / total_cells)[:, None]).astype(jnp.bfloat16), "sub").astype(
        jnp.float32
    )
    basis = (wide * scale[:, None]).astype(jnp.bfloat16)
    return (basis[None], gram)


def solution(mesh):
    return jax.shard_map(
        body,
        mesh=mesh,
        in_specs=(
            P("sub", "blk", None),
            P("sub", "blk", None),
            P("sub", "blk", None),
            P("sub", None, None),
            P("sub", None, None),
        ),
        out_specs=(P("sub", "blk", None), P("blk", None)),
        check_vma=False,
    )
```

```python
import functools

import jax
import jax.numpy as jnp
from jax import lax
from jax.experimental import pallas as pl
from jax.experimental.pallas import tpu as pltpu
from jax.sharding import PartitionSpec as P

MESH = pl.DeviceIdType.MESH
UNKNOWNS = 3072
SHOTS = 512
BLOCK = 384
HALF = BLOCK // 2
BLOCKS = UNKNOWNS // BLOCK
RINGS = 4
PIECES = 4
PIECE = SHOTS // PIECES
MARGIN = 512
GROUP = 16
SHARE = SHOTS // GROUP


def times_rows(left, right):
    return lax.dot_general(
        left, right, (((1,), (1,)), ((), ())), preferred_element_type=jnp.float32
    )


def columns(k):
    return pl.ds(pl.multiple_of(k * BLOCK, BLOCK), BLOCK)


def solve_kernel(
    rhs_in,
    lower_in,
    upper_in,
    out,
    rhs,
    lower,
    upper,
    interim,
    local,
    own_sem,
    x_recv,
    x_send,
    r_recv,
    r_send,
    near_recv,
    near_send,
    far_recv,
    far_send,
    sib_recv,
    sib_send,
    ret_recv,
    ret_send,
    out_sem,
):
    sub = lax.axis_index("sub")
    blk = lax.axis_index("blk")
    core = sub % 2
    pair = sub - core
    half = blk // RINGS
    y = blk % RINGS
    guest = core != half
    home = core == half
    partner = (pair + 1 - core, (1 - half) * RINGS + y)
    sibling = (pair + 1 - core, blk)
    up = (sub, half * RINGS + (y + 1) % RINGS)
    down = (sub, half * RINGS + (y + 3) % RINGS)
    mine = core * RINGS + y
    below = core * RINGS + (y + 3) % RINGS
    above = core * RINGS + (y + 1) % RINGS
    across = core * RINGS + (y + 2) % RINGS

    barrier = pltpu.get_barrier_semaphore()
    for other in (partner, sibling, up, down):
        pl.semaphore_signal(barrier, inc=1, device_id=other, device_id_type=MESH)
    pl.semaphore_wait(barrier, 4)

    sources = (lower_in, upper_in)
    holds = (lower, upper)

    def span(w, b):
        return (0, b + 1) if w == 0 else (b, BLOCKS)

    def remote(src, dst, send, recv, device):
        return pltpu.make_async_remote_copy(
            src_ref=src,
            dst_ref=dst,
            send_sem=send,
            recv_sem=recv,
            device_id=device,
            device_id_type=MESH,
        )

    def whole(w, b, k):
        return holds[w].at[b, :, columns(k)]

    def part(w, b, k, top):
        return holds[w].at[b, pl.ds(0 if top else HALF, HALF), columns(k)]

    def exchange(w, k):
        return remote(
            sources[w].at[0, :, columns(k)],
            whole(w, blk, k),
            x_send.at[w, k],
            x_recv.at[w, k],
            partner,
        )

    def exchange_rhs(i):
        rows = pl.ds(i * PIECE, PIECE)
        return remote(rhs_in.at[0, rows], rhs.at[rows], r_send.at[i], r_recv.at[i], partner)

    def to_near(w, k, upward, src):
        d = 0 if upward else 1
        return remote(
            src,
            whole(w, mine, k),
            near_send.at[w, d, k],
            near_recv.at[w, d, k],
            up if upward else down,
        )

    def to_far(w, b, k, upward):
        d = 0 if upward else 1
        return remote(
            part(w, b, k, upward),
            part(w, b, k, upward),
            far_send.at[w, d, k],
            far_recv.at[w, d, k],
            up if upward else down,
        )

    def to_sibling(w, b, slot, k, src):
        return remote(
            src,
            whole(w, b, k),
            sib_send.at[w, slot, k],
            sib_recv.at[w, slot, k],
            sibling,
        )

    def each(w, b, step):
        first, last = span(w, b)

        def go(k, carry):
            step(k)
            return carry

        lax.fori_loop(first, last, go, 0)

    def send_own(w, src):
        def step(k):
            to_near(w, k, True, src(k)).start()
            to_near(w, k, False, src(k)).start()
            to_sibling(w, mine, 0, k, src(k)).start()

        return step

    def own_from_input(w):
        each(w, mine, send_own(w, lambda k: sources[w].at[0, :, columns(k)]))

    def own_from_partner(w):
        send = send_own(w, lambda k: whole(w, mine, k))

        def step(k):
            remote(
                whole(w, mine, k), whole(w, mine, k), x_send.at[w, k], x_recv.at[w, k], partner
            ).wait_recv()
            send(k)

        each(w, mine, step)

    def relay_from(w, upward, k):
        b = below if upward else above
        d = 0 if upward else 1
        remote(
            whole(w, b, k),
            whole(w, b, k),
            near_send.at[w, d, k],
            near_recv.at[w, d, k],
            up if upward else down,
        ).wait_recv()
        to_far(w, b, k, upward).start()
        to_sibling(w, b, 1 + d, k, whole(w, b, k)).start()

    def relay(w, j):
        for upward, b in ((True, below), (False, above)):
            first, last = span(w, b)

            @pl.when(first + j < last)
            def _():
                relay_from(w, upward, first + j)

    def relay_all(w):
        def go(j, carry):
            relay(w, j)
            return carry

        lax.fori_loop(0, BLOCKS, go, 0)

    def relay_across(w):
        def step(k):
            for upward in (True, False):
                to_far(w, across, k, upward).wait_recv()
            to_sibling(w, across, 3, k, whole(w, across, k)).start()

        each(w, across, step)

    def own_copy(w):
        return pltpu.make_async_copy(sources[w].at[0], holds[w].at[mine], own_sem.at[w])

    def rhs_copy():
        return pltpu.make_async_copy(rhs_in.at[0], rhs, own_sem.at[2])

    def turn(t):
        i = t % RINGS
        return jnp.where(i == 0, 0, jnp.where(i == 1, 3, i - 1))

    def from_sibling(w, slot):
        b = (1 - core) * RINGS + (y + turn(slot)) % RINGS

        def step(k):
            to_sibling(w, b, slot, k, whole(w, b, k)).wait_recv()

        each(w, b, step)

    @pl.when(home)
    def _():
        own_from_input(0)
        rhs_copy().start()
        own_copy(0).start()
        own_copy(1).start()
        relay_all(0)
        own_from_input(1)
        relay_across(0)
        relay_all(1)
        relay_across(1)
        rhs_copy().wait()
        own_copy(0).wait()
        own_copy(1).wait()

    @pl.when(guest)
    def _():
        each(0, blk, lambda k: exchange(0, k).start())
        own_from_partner(0)
        for i in range(PIECES):
            exchange_rhs(i).start()
        relay_all(0)
        relay_across(0)
        each(1, blk, lambda k: exchange(1, k).start())
        for i in range(PIECES):
            exchange_rhs(i).wait_recv()

    def wait_lower(slot, carry):
        from_sibling(0, slot)
        return carry

    lax.fori_loop(0, RINGS, wait_lower, 0)

    for b in range(BLOCKS):
        stop = (b + 1) * BLOCK
        interim[:, b * BLOCK : stop] = times_rows(rhs[:, :stop], lower[b, :, :stop]).astype(
            jnp.bfloat16
        )

    @pl.when(guest)
    def _():
        own_from_partner(1)

    def back(b):
        return remote(
            local.at[:, columns(b)],
            out.at[:, columns(b)],
            ret_send.at[b],
            ret_recv.at[b],
            partner,
        )

    def keep(b):
        return pltpu.make_async_copy(
            local.at[:, columns(b)], out.at[:, columns(b)], out_sem.at[b]
        )

    def solve_step(t, carry):
        ring = jnp.where(t < RINGS, half, 1 - half)

        @pl.when(guest & (t < RINGS))
        def _():
            relay(1, 2 * t)
            relay(1, 2 * t + 1)

        @pl.when(guest & (t == 2 * RINGS - 1))
        def _():
            relay_across(1)

        @pl.when(ring != core)
        def _():
            from_sibling(1, t % RINGS)

        block = ring * RINGS + (y + turn(t)) % RINGS
        for b in range(BLOCKS):

            @pl.when(block == b)
            def _():
                start = b * BLOCK
                local[:, start : start + BLOCK] = times_rows(
                    interim[:, start:], upper[b, :, start:]
                ).astype(jnp.bfloat16)

        @pl.when(guest)
        def _():
            back(block).start()

        @pl.when(home)
        def _():
            keep(block).start()

        return carry

    lax.fori_loop(0, BLOCKS, solve_step, 0)

    for w in range(2):

        def own_sent(k):
            to_near(w, k, True, whole(w, mine, k)).wait_send()
            to_near(w, k, False, whole(w, mine, k)).wait_send()
            to_sibling(w, mine, 0, k, whole(w, mine, k)).wait_send()

        each(w, mine, own_sent)
        for upward, b in ((True, below), (False, above)):
            slot = 1 if upward else 2

            def near_sent(k):
                to_far(w, b, k, upward).wait_send()
                to_sibling(w, b, slot, k, whole(w, b, k)).wait_send()

            each(w, b, near_sent)
        each(w, across, lambda k: to_sibling(w, across, 3, k, whole(w, across, k)).wait_send())

        @pl.when(guest)
        def _():
            each(w, blk, lambda k: exchange(w, k).wait_send())

    @pl.when(guest)
    def _():
        for i in range(PIECES):
            exchange_rhs(i).wait_send()

    def finish(b, carry):
        @pl.when(guest)
        def _():
            back(b).wait()

        @pl.when(home)
        def _():
            keep(b).wait()

        return carry

    lax.fori_loop(0, BLOCKS, finish, 0)


def solve(residual, lower_factor, upper_factor):
    dma = pltpu.SemaphoreType.DMA
    hbm = pl.BlockSpec(memory_space=pl.ANY)
    return pl.pallas_call(
        solve_kernel,
        out_shape=jax.ShapeDtypeStruct((SHOTS, UNKNOWNS), jnp.bfloat16),
        in_specs=[hbm] * 3,
        out_specs=hbm,
        scratch_shapes=[
            pltpu.VMEM((SHOTS, UNKNOWNS), jnp.bfloat16),
            pltpu.VMEM((BLOCKS, BLOCK, UNKNOWNS), jnp.bfloat16),
            pltpu.VMEM((BLOCKS, BLOCK, UNKNOWNS), jnp.bfloat16),
            pltpu.VMEM((SHOTS, UNKNOWNS), jnp.bfloat16),
            pltpu.VMEM((SHOTS, UNKNOWNS), jnp.bfloat16),
            dma((3,)),
            dma((2, BLOCKS)),
            dma((2, BLOCKS)),
            dma((PIECES,)),
            dma((PIECES,)),
            dma((2, 2, BLOCKS)),
            dma((2, 2, BLOCKS)),
            dma((2, 2, BLOCKS)),
            dma((2, 2, BLOCKS)),
            dma((2, RINGS, BLOCKS)),
            dma((2, RINGS, BLOCKS)),
            dma((BLOCKS,)),
            dma((BLOCKS,)),
            dma((BLOCKS,)),
        ],
        compiler_params=pltpu.CompilerParams(
            collective_id=0, has_side_effects=True, vmem_limit_bytes=60 * 1024 * 1024
        ),
        cost_estimate=pl.CostEstimate(
            flops=2 * 36 * 2 * SHOTS * BLOCK * BLOCK,
            bytes_accessed=5 * SHOTS * UNKNOWNS * 2,
            transcendentals=0,
        ),
    )(residual, lower_factor, upper_factor)


def finish_kernel(
    cells,
    local_in,
    rhs_in,
    rows_in,
    blend_in,
    blended_out,
    scale_out,
    gram_out,
    local,
    rhs,
    picks,
    kept,
    at,
    fresh,
    neighbour,
    rhs_at,
    raw,
    outgoing,
    incoming,
    reduced,
    blended,
    scale,
    mask,
    squares,
    load_sem,
    store_sem,
    side_send,
    side_recv,
    sq_send,
    sq_recv,
    raw_send,
    raw_recv,
    gram_send,
    gram_recv,
):
    sub = lax.axis_index("sub")
    blk = lax.axis_index("blk")

    def mate(d):
        return ((sub + d) % GROUP, blk)

    def remote(src, dst, send, recv, device):
        return pltpu.make_async_remote_copy(
            src_ref=src,
            dst_ref=dst,
            send_sem=send,
            recv_sem=recv,
            device_id=device,
            device_id_type=MESH,
        )

    def each_mate(step):
        def go(d, carry):
            step(d)
            return carry

        lax.fori_loop(1, GROUP, go, 0)

    barrier = pltpu.get_barrier_semaphore()
    each_mate(
        lambda d: pl.semaphore_signal(barrier, inc=1, device_id=mate(d), device_id_type=MESH)
    )
    load_local = pltpu.make_async_copy(local_in, local, load_sem.at[0])
    load_rhs = pltpu.make_async_copy(rhs_in.at[0], rhs, load_sem.at[1])
    load_local.start()
    load_rhs.start()

    def pick(i, carry):
        place = pl.ds(pl.multiple_of(i * 256, 256), 256)
        unknown = lax.broadcasted_iota(jnp.int32, (256, MARGIN), 0) + i * 256
        for side in range(2):
            hit = unknown == rows_in[0, side : side + 1, :]
            picks[place, side * MARGIN : (side + 1) * MARGIN] = jnp.where(
                hit, jnp.float32(1), jnp.float32(0)
            ).astype(jnp.bfloat16)
        return carry

    lax.fori_loop(0, UNKNOWNS // 256, pick, 0)
    load_local.wait()
    pl.semaphore_wait(barrier, GROUP - 1)

    def picked(values):
        return lambda lanes: jnp.dot(
            values[...], picks[:, lanes], preferred_element_type=jnp.float32
        ).astype(jnp.bfloat16)

    def side_copy(side):
        return remote(
            at.at[side],
            neighbour.at[1 - side],
            side_send.at[side],
            side_recv.at[1 - side],
            ((sub + (GROUP - 1 if side == 0 else 1)) % GROUP, blk),
        )

    lasting = (sub > 0, sub < GROUP - 1)

    for side in range(2):
        at_side = picked(local)
        for lanes in range(0, MARGIN, 256):
            at[side, :, lanes : lanes + 256] = at_side(
                slice(side * MARGIN + lanes, side * MARGIN + lanes + 256)
            )

        @pl.when(lasting[side])
        def _():
            side_copy(side).start()

    mask[...] = times_rows(jnp.ones((16, 2 * MARGIN), jnp.bfloat16), picks[...])

    def keep_rows(i, carry):
        place = pl.ds(pl.multiple_of(i * 64, 64), 64)
        rest = jnp.where(mask[0:1, :] > 0.5, 0.0, local[place, :].astype(jnp.float32))
        kept[place, :] = rest.astype(jnp.bfloat16)
        total = jnp.zeros((64, 128), jnp.float32)
        for lane in range(0, UNKNOWNS, 128):
            piece = rest[:, lane : lane + 128]
            total += piece * piece
        scale[place, :] = total
        return carry

    lax.fori_loop(0, SHOTS // 64, keep_rows, 0)
    load_rhs.wait()
    at_rhs = picked(rhs)
    for lanes in range(0, 2 * MARGIN, 256):
        rhs_at[:, lanes : lanes + 256] = at_rhs(slice(lanes, lanes + 256))
    for lanes in range(0, SHOTS, 256):
        raw[:, lanes : lanes + 256] = times_rows(kept[...], rhs[lanes : lanes + 256, :])

    for side in range(2):
        lanes = slice(side * MARGIN, (side + 1) * MARGIN)

        @pl.when(lasting[side])
        def _():
            side_copy(1 - side).wait_recv()
            value = at[side].astype(jnp.float32)
            other = neighbour[side].astype(jnp.float32)
            fresh[:, lanes] = (
                value + blend_in[0, side : side + 1, :] * (other - value)
            ).astype(jnp.bfloat16)

        @pl.when(jnp.logical_not(lasting[side]))
        def _():
            fresh[:, lanes] = at[side]

    total = scale[...]
    for lane in range(0, 2 * MARGIN, 128):
        piece = fresh[:, lane : lane + 128].astype(jnp.float32)
        total += piece * piece
    across = jnp.sum(total.T, axis=0, keepdims=True)
    squares[0] = jnp.zeros((8, 128), jnp.float32)
    for i in range(SHOTS // 128):
        squares[0, i : i + 1, :] = across[:, i * 128 : (i + 1) * 128]

    def sq_copy(d):
        return remote(squares.at[0], squares.at[d], sq_send.at[d], sq_recv.at[d], mate(d))

    each_mate(lambda d: sq_copy(d).start())

    outgoing[...] = (raw[...] + times_rows(fresh[...], rhs_at[...])).astype(jnp.bfloat16)

    def own_rows(who):
        return pl.ds(pl.multiple_of(who * SHARE, SHARE), SHARE)

    def raw_copy(d):
        return remote(
            outgoing.at[own_rows((sub + d) % GROUP)],
            incoming.at[d],
            raw_send.at[d],
            raw_recv.at[d],
            mate(d),
        )

    each_mate(lambda d: raw_copy(d).start())

    for lane in range(0, UNKNOWNS, BLOCK):
        lanes = slice(lane, lane + BLOCK)
        placed = times_rows(fresh[...], picks[lanes, :])
        blended[:, lanes] = jnp.where(
            mask[0:1, lanes] > 0.5, placed, local[:, lanes].astype(jnp.float32)
        ).astype(jnp.bfloat16)
    store_blended = pltpu.make_async_copy(blended, blended_out, store_sem.at[0])
    store_blended.start()

    each_mate(lambda d: sq_copy(d).wait_recv())
    grand = squares[0]
    for d in range(1, GROUP):
        grand += squares[d]
    factor = 1.0 / jnp.sqrt(grand / cells + 1e-05)
    for i in range(SHOTS // 128):
        scale[i * 128 : (i + 1) * 128, :] = jnp.broadcast_to(factor[i : i + 1, :], (128, 128)).T
    store_scale = pltpu.make_async_copy(scale, scale_out, store_sem.at[1])
    store_scale.start()

    each_mate(lambda d: raw_copy(d).wait_recv())
    sum_rows = outgoing[own_rows(sub), :].astype(jnp.float32)
    for d in range(1, GROUP):
        sum_rows += incoming[d].astype(jnp.float32)
    reduced[...] = (sum_rows * (scale[own_rows(sub), 0:1] / cells)).astype(jnp.bfloat16)

    def gram_copy(d):
        return remote(
            reduced,
            gram_out.at[own_rows(sub)],
            gram_send.at[d],
            gram_recv.at[d],
            mate(d),
        )

    store_gram = pltpu.make_async_copy(reduced, gram_out.at[own_rows(sub)], store_sem.at[2])
    store_gram.start()
    each_mate(lambda d: gram_copy(d).start())

    each_mate(lambda d: gram_copy(d).wait_recv())
    for side in range(2):

        @pl.when(lasting[side])
        def _():
            side_copy(side).wait_send()

    each_mate(lambda d: sq_copy(d).wait_send())
    each_mate(lambda d: raw_copy(d).wait_send())
    each_mate(lambda d: gram_copy(d).wait_send())
    store_blended.wait()
    store_scale.wait()
    store_gram.wait()


def finish(local, residual, margin_rows, blend):
    dma = pltpu.SemaphoreType.DMA
    hbm = pl.BlockSpec(memory_space=pl.ANY)
    vmem = pl.BlockSpec(memory_space=pltpu.VMEM)
    bf16 = jnp.bfloat16
    return pl.pallas_call(
        functools.partial(finish_kernel, float(GROUP * UNKNOWNS)),
        out_shape=(
            jax.ShapeDtypeStruct((SHOTS, UNKNOWNS), bf16),
            jax.ShapeDtypeStruct((SHOTS, 128), jnp.float32),
            jax.ShapeDtypeStruct((SHOTS, SHOTS), bf16),
        ),
        in_specs=[hbm, hbm, vmem, vmem],
        out_specs=(hbm, hbm, hbm),
        scratch_shapes=[
            pltpu.VMEM((SHOTS, UNKNOWNS), bf16),
            pltpu.VMEM((SHOTS, UNKNOWNS), bf16),
            pltpu.VMEM((UNKNOWNS, 2 * MARGIN), bf16),
            pltpu.VMEM((SHOTS, UNKNOWNS), bf16),
            pltpu.VMEM((2, SHOTS, MARGIN), bf16),
            pltpu.VMEM((SHOTS, 2 * MARGIN), bf16),
            pltpu.VMEM((2, SHOTS, MARGIN), bf16),
            pltpu.VMEM((SHOTS, 2 * MARGIN), bf16),
            pltpu.VMEM((SHOTS, SHOTS), jnp.float32),
            pltpu.VMEM((SHOTS, SHOTS), bf16),
            pltpu.VMEM((GROUP, SHARE, SHOTS), bf16),
            pltpu.VMEM((SHARE, SHOTS), bf16),
            pltpu.VMEM((SHOTS, UNKNOWNS), bf16),
            pltpu.VMEM((SHOTS, 128), jnp.float32),
            pltpu.VMEM((16, UNKNOWNS), jnp.float32),
            pltpu.VMEM((GROUP, 8, 128), jnp.float32),
            dma((2,)),
            dma((3,)),
            dma((2,)),
            dma((2,)),
            dma((GROUP,)),
            dma((GROUP,)),
            dma((GROUP,)),
            dma((GROUP,)),
            dma((GROUP,)),
            dma((GROUP,)),
        ],
        compiler_params=pltpu.CompilerParams(
            collective_id=1, has_side_effects=True, vmem_limit_bytes=60 * 1024 * 1024
        ),
    )(local, residual, margin_rows, blend)


def body(residual, lower_factor, upper_factor, margin_rows, blend):
    local = solve(residual, lower_factor, upper_factor)
    blended, scale, gram = finish(local, residual, margin_rows, blend)
    basis = (blended.astype(jnp.float32) * scale[:, :1]).astype(jnp.bfloat16)
    return (basis[None], gram.astype(jnp.float32))


def solution(mesh):
    return jax.shard_map(
        body,
        mesh=mesh,
        in_specs=(
            P("sub", "blk", None),
            P("sub", "blk", None),
            P("sub", "blk", None),
            P("sub", None, None),
            P("sub", None, None),
        ),
        out_specs=(P("sub", "blk", None), P("blk", None)),
        check_vma=False,
    )
```

```python
import functools

import jax
import jax.numpy as jnp
from jax import lax
from jax.experimental import pallas as pl
from jax.experimental.pallas import tpu as pltpu
from jax.sharding import PartitionSpec as P

MESH = pl.DeviceIdType.MESH
UNKNOWNS = 3072
SHOTS = 512
BLOCK = 384
HALF = BLOCK // 2
BLOCKS = UNKNOWNS // BLOCK
RINGS = 4
PIECES = 4
PIECE = SHOTS // PIECES
MARGIN = 512
GROUP = 16
SHARE = SHOTS // GROUP


def times_rows(left, right):
    return lax.dot_general(
        left, right, (((1,), (1,)), ((), ())), preferred_element_type=jnp.float32
    )


def columns(k):
    return pl.ds(pl.multiple_of(k * BLOCK, BLOCK), BLOCK)


def solve_kernel(
    rhs_in,
    lower_in,
    upper_in,
    out,
    rhs,
    lower,
    upper,
    interim,
    local,
    own_sem,
    x_recv,
    x_send,
    r_recv,
    r_send,
    near_recv,
    near_send,
    far_recv,
    far_send,
    sib_recv,
    sib_send,
    ret_recv,
    ret_send,
    out_sem,
):
    sub = lax.axis_index("sub")
    blk = lax.axis_index("blk")
    core = sub % 2
    pair = sub - core
    half = blk // RINGS
    y = blk % RINGS
    guest = core != half
    home = core == half
    partner = (pair + 1 - core, (1 - half) * RINGS + y)
    sibling = (pair + 1 - core, blk)
    up = (sub, half * RINGS + (y + 1) % RINGS)
    down = (sub, half * RINGS + (y + 3) % RINGS)
    opposite = (sub, (1 - half) * RINGS + y)

    barrier = pltpu.get_barrier_semaphore()
    for other in (partner, opposite, sibling, up, down):
        pl.semaphore_signal(barrier, inc=1, device_id=other, device_id_type=MESH)
    pl.semaphore_wait(barrier, 5)

    sources = (lower_in, upper_in)
    holds = (lower, upper)
    factor = (0, 1, 1)
    ring = (core, half, 1 - half)

    def block(v, offset):
        return ring[v] * RINGS + (y + offset) % RINGS

    def span(w, b):
        return (0, b + 1) if w == 0 else (b, BLOCKS)

    def remote(src, dst, send, recv, device):
        return pltpu.make_async_remote_copy(
            src_ref=src,
            dst_ref=dst,
            send_sem=send,
            recv_sem=recv,
            device_id=device,
            device_id_type=MESH,
        )

    def whole(v, b, k):
        return holds[factor[v]].at[b, :, columns(k)]

    def part(v, b, k, top):
        return holds[factor[v]].at[b, pl.ds(0 if top else HALF, HALF), columns(k)]

    def exchange(w, k):
        return remote(
            sources[w].at[0, :, columns(k)],
            whole(w, blk, k),
            x_send.at[w, k],
            x_recv.at[w, k],
            partner if w == 0 else opposite,
        )

    def exchange_rhs(i):
        rows = pl.ds(i * PIECE, PIECE)
        return remote(rhs_in.at[0, rows], rhs.at[rows], r_send.at[i], r_recv.at[i], partner)

    def to_near(v, k, upward, src):
        d = 0 if upward else 1
        return remote(
            src,
            whole(v, block(v, 0), k),
            near_send.at[v, d, k],
            near_recv.at[v, d, k],
            up if upward else down,
        )

    def to_far(v, b, k, upward):
        d = 0 if upward else 1
        return remote(
            part(v, b, k, upward),
            part(v, b, k, upward),
            far_send.at[v, d, k],
            far_recv.at[v, d, k],
            up if upward else down,
        )

    def to_sibling(v, b, slot, k, src):
        return remote(
            src,
            whole(v, b, k),
            sib_send.at[v, slot, k],
            sib_recv.at[v, slot, k],
            sibling,
        )

    def each(v, b, step):
        first, last = span(factor[v], b)

        def go(k, carry):
            step(k)
            return carry

        lax.fori_loop(first, last, go, 0)

    def send_own(v, k, src):
        to_near(v, k, True, src).start()
        to_near(v, k, False, src).start()
        to_sibling(v, block(v, 0), 0, k, src).start()

    def own_from_input(v):
        each(
            v,
            block(v, 0),
            lambda k: send_own(v, k, sources[factor[v]].at[0, :, columns(k)]),
        )

    def own_from_partner(v):
        def step(k):
            here = whole(v, block(v, 0), k)
            w = factor[v]
            remote(here, here, x_send.at[w, k], x_recv.at[w, k], partner).wait_recv()
            send_own(v, k, here)

        each(v, block(v, 0), step)

    def relay_from(v, upward, k):
        d = 0 if upward else 1
        b = block(v, 3 if upward else 1)
        here = whole(v, b, k)
        remote(
            here, here, near_send.at[v, d, k], near_recv.at[v, d, k], up if upward else down
        ).wait_recv()
        to_far(v, b, k, upward).start()
        to_sibling(v, b, 1 + d, k, here).start()

    def relay_near(v):
        def go(j, carry):
            for upward in (True, False):
                first, last = span(factor[v], block(v, 3 if upward else 1))

                @pl.when(first + j < last)
                def _():
                    relay_from(v, upward, first + j)

            return carry

        lax.fori_loop(0, BLOCKS, go, 0)

    def relay_across(v):
        b = block(v, 2)

        def step(k):
            for upward in (True, False):
                to_far(v, b, k, upward).wait_recv()
            to_sibling(v, b, 3, k, whole(v, b, k)).start()

        each(v, b, step)

    def own_copy(w):
        return pltpu.make_async_copy(sources[w].at[0], holds[w].at[blk], own_sem.at[w])

    def rhs_copy():
        return pltpu.make_async_copy(rhs_in.at[0], rhs, own_sem.at[2])

    def turn(t):
        return jnp.where(t == 0, 0, jnp.where(t == 1, 3, t - 1))

    def from_sibling(v, b, slot):
        each(v, b, lambda k: to_sibling(v, b, slot, k, whole(v, b, k)).wait_recv())

    def lower_from_sibling(slot):
        from_sibling(0, (1 - core) * RINGS + (y + turn(slot)) % RINGS, slot)

    @pl.when(home)
    def _():
        own_from_input(0)
        rhs_copy().start()
        own_copy(0).start()
        own_copy(1).start()
        relay_near(0)
        lower_from_sibling(0)
        own_from_input(1)
        relay_across(0)
        own_from_partner(2)
        lower_from_sibling(1)
        lower_from_sibling(2)
        relay_near(1)
        rhs_copy().wait()
        own_copy(0).wait()
        own_copy(1).wait()

    @pl.when(guest)
    def _():
        each(0, blk, lambda k: exchange(0, k).start())
        own_from_partner(0)
        for i in range(PIECES):
            exchange_rhs(i).start()
        each(1, blk, lambda k: exchange(1, k).start())
        relay_near(0)
        relay_across(0)
        for i in range(PIECES):
            exchange_rhs(i).wait_recv()
        lower_from_sibling(0)
        lower_from_sibling(1)
        lower_from_sibling(2)

    lower_from_sibling(3)

    for b in range(BLOCKS):
        stop = (b + 1) * BLOCK
        interim[:, b * BLOCK : stop] = (
            times_rows(lower[b, :, :stop], rhs[:, :stop]).astype(jnp.bfloat16).T
        )

    @pl.when(home)
    def _():
        relay_near(2)
        relay_across(1)

    def back(b):
        return remote(
            local.at[:, columns(b)],
            out.at[:, columns(b)],
            ret_send.at[b],
            ret_recv.at[b],
            partner,
        )

    def keep(b):
        return pltpu.make_async_copy(
            local.at[:, columns(b)], out.at[:, columns(b)], out_sem.at[b]
        )

    def solve_step(t, carry):
        first_half = (t == 0) | (t == 2) | (t == 3) | (t == 6)
        slot = jnp.where(t < 2, 0, jnp.where(t > 5, 3, 1 + t % 2))
        this = jnp.where(first_half, half, 1 - half) * RINGS + (y + turn(slot)) % RINGS

        @pl.when(home & (t == 6))
        def _():
            relay_across(2)

        @pl.when(guest & first_half)
        def _():
            from_sibling(1, this, slot)

        @pl.when(guest & jnp.logical_not(first_half))
        def _():
            from_sibling(2, this, slot)

        for b in range(BLOCKS):

            @pl.when(this == b)
            def _():
                start = b * BLOCK
                local[:, start : start + BLOCK] = (
                    times_rows(upper[b, :, start:], interim[:, start:]).astype(jnp.bfloat16).T
                )

        @pl.when(guest)
        def _():
            back(this).start()

        @pl.when(home)
        def _():
            keep(this).start()

        return carry

    lax.fori_loop(0, BLOCKS, solve_step, 0)

    def sent(v):
        def own_sent(k):
            here = whole(v, block(v, 0), k)
            to_near(v, k, True, here).wait_send()
            to_near(v, k, False, here).wait_send()
            to_sibling(v, block(v, 0), 0, k, here).wait_send()

        each(v, block(v, 0), own_sent)
        for upward in (True, False):
            b = block(v, 3 if upward else 1)

            def near_sent(k):
                to_far(v, b, k, upward).wait_send()
                to_sibling(v, b, 1 if upward else 2, k, whole(v, b, k)).wait_send()

            each(v, b, near_sent)
        b = block(v, 2)
        each(v, b, lambda k: to_sibling(v, b, 3, k, whole(v, b, k)).wait_send())

    sent(0)

    @pl.when(home)
    def _():
        sent(1)
        sent(2)

    @pl.when(guest)
    def _():
        for w in range(2):
            each(w, blk, lambda k: exchange(w, k).wait_send())
        for i in range(PIECES):
            exchange_rhs(i).wait_send()

    def finish(b, carry):
        @pl.when(guest)
        def _():
            back(b).wait()

        @pl.when(home)
        def _():
            keep(b).wait()

        return carry

    lax.fori_loop(0, BLOCKS, finish, 0)


def solve(residual, lower_factor, upper_factor):
    dma = pltpu.SemaphoreType.DMA
    hbm = pl.BlockSpec(memory_space=pl.ANY)
    return pl.pallas_call(
        solve_kernel,
        out_shape=jax.ShapeDtypeStruct((SHOTS, UNKNOWNS), jnp.bfloat16),
        in_specs=[hbm] * 3,
        out_specs=hbm,
        scratch_shapes=[
            pltpu.VMEM((SHOTS, UNKNOWNS), jnp.bfloat16),
            pltpu.VMEM((BLOCKS, BLOCK, UNKNOWNS), jnp.bfloat16),
            pltpu.VMEM((BLOCKS, BLOCK, UNKNOWNS), jnp.bfloat16),
            pltpu.VMEM((SHOTS, UNKNOWNS), jnp.bfloat16),
            pltpu.VMEM((SHOTS, UNKNOWNS), jnp.bfloat16),
            dma((3,)),
            dma((2, BLOCKS)),
            dma((2, BLOCKS)),
            dma((PIECES,)),
            dma((PIECES,)),
            dma((3, 2, BLOCKS)),
            dma((3, 2, BLOCKS)),
            dma((3, 2, BLOCKS)),
            dma((3, 2, BLOCKS)),
            dma((3, RINGS, BLOCKS)),
            dma((3, RINGS, BLOCKS)),
            dma((BLOCKS,)),
            dma((BLOCKS,)),
            dma((BLOCKS,)),
        ],
        compiler_params=pltpu.CompilerParams(
            collective_id=0, has_side_effects=True, vmem_limit_bytes=60 * 1024 * 1024
        ),
        cost_estimate=pl.CostEstimate(
            flops=2 * 36 * 2 * SHOTS * BLOCK * BLOCK,
            bytes_accessed=5 * SHOTS * UNKNOWNS * 2,
            transcendentals=0,
        ),
    )(residual, lower_factor, upper_factor)


def finish_kernel(
    cells,
    local_in,
    rhs_in,
    rows_in,
    blend_in,
    blended_out,
    scale_out,
    gram_out,
    local,
    rhs,
    picks,
    kept,
    at,
    fresh,
    neighbour,
    rhs_at,
    raw,
    outgoing,
    incoming,
    reduced,
    blended,
    scale,
    mask,
    squares,
    load_sem,
    store_sem,
    side_send,
    side_recv,
    sq_send,
    sq_recv,
    raw_send,
    raw_recv,
    gram_send,
    gram_recv,
):
    sub = lax.axis_index("sub")
    blk = lax.axis_index("blk")

    def mate(d):
        return ((sub + d) % GROUP, blk)

    def remote(src, dst, send, recv, device):
        return pltpu.make_async_remote_copy(
            src_ref=src,
            dst_ref=dst,
            send_sem=send,
            recv_sem=recv,
            device_id=device,
            device_id_type=MESH,
        )

    def each_mate(step):
        def go(d, carry):
            step(d)
            return carry

        lax.fori_loop(1, GROUP, go, 0)

    barrier = pltpu.get_barrier_semaphore()
    each_mate(
        lambda d: pl.semaphore_signal(barrier, inc=1, device_id=mate(d), device_id_type=MESH)
    )
    load_local = pltpu.make_async_copy(local_in, local, load_sem.at[0])
    load_rhs = pltpu.make_async_copy(rhs_in.at[0], rhs, load_sem.at[1])
    load_local.start()
    load_rhs.start()

    def pick(i, carry):
        place = pl.ds(pl.multiple_of(i * 256, 256), 256)
        unknown = lax.broadcasted_iota(jnp.int32, (256, MARGIN), 0) + i * 256
        for side in range(2):
            hit = unknown == rows_in[0, side : side + 1, :]
            picks[place, side * MARGIN : (side + 1) * MARGIN] = jnp.where(
                hit, jnp.float32(1), jnp.float32(0)
            ).astype(jnp.bfloat16)
        return carry

    lax.fori_loop(0, UNKNOWNS // 256, pick, 0)
    load_local.wait()
    pl.semaphore_wait(barrier, GROUP - 1)

    def picked(values):
        return lambda lanes: jnp.dot(
            values[...], picks[:, lanes], preferred_element_type=jnp.float32
        ).astype(jnp.bfloat16)

    def side_copy(side):
        return remote(
            at.at[side],
            neighbour.at[1 - side],
            side_send.at[side],
            side_recv.at[1 - side],
            ((sub + (GROUP - 1 if side == 0 else 1)) % GROUP, blk),
        )

    lasting = (sub > 0, sub < GROUP - 1)

    for side in range(2):
        at_side = picked(local)
        for lanes in range(0, MARGIN, 256):
            at[side, :, lanes : lanes + 256] = at_side(
                slice(side * MARGIN + lanes, side * MARGIN + lanes + 256)
            )

        @pl.when(lasting[side])
        def _():
            side_copy(side).start()

    mask[...] = times_rows(jnp.ones((16, 2 * MARGIN), jnp.bfloat16), picks[...])

    def keep_rows(i, carry):
        place = pl.ds(pl.multiple_of(i * 64, 64), 64)
        rest = jnp.where(mask[0:1, :] > 0.5, 0.0, local[place, :].astype(jnp.float32))
        kept[place, :] = rest.astype(jnp.bfloat16)
        total = jnp.zeros((64, 128), jnp.float32)
        for lane in range(0, UNKNOWNS, 128):
            piece = rest[:, lane : lane + 128]
            total += piece * piece
        scale[place, :] = total
        return carry

    lax.fori_loop(0, SHOTS // 64, keep_rows, 0)
    load_rhs.wait()
    at_rhs = picked(rhs)
    for lanes in range(0, 2 * MARGIN, 256):
        rhs_at[:, lanes : lanes + 256] = at_rhs(slice(lanes, lanes + 256))
    for lanes in range(0, SHOTS, 256):
        raw[:, lanes : lanes + 256] = times_rows(kept[...], rhs[lanes : lanes + 256, :])

    for side in range(2):
        lanes = slice(side * MARGIN, (side + 1) * MARGIN)

        @pl.when(lasting[side])
        def _():
            side_copy(1 - side).wait_recv()
            value = at[side].astype(jnp.float32)
            other = neighbour[side].astype(jnp.float32)
            fresh[:, lanes] = (
                value + blend_in[0, side : side + 1, :] * (other - value)
            ).astype(jnp.bfloat16)

        @pl.when(jnp.logical_not(lasting[side]))
        def _():
            fresh[:, lanes] = at[side]

    total = scale[...]
    for lane in range(0, 2 * MARGIN, 128):
        piece = fresh[:, lane : lane + 128].astype(jnp.float32)
        total += piece * piece
    across = jnp.sum(total.T, axis=0, keepdims=True)
    squares[0] = jnp.zeros((8, 128), jnp.float32)
    for i in range(SHOTS // 128):
        squares[0, i : i + 1, :] = across[:, i * 128 : (i + 1) * 128]

    def sq_copy(d):
        return remote(squares.at[0], squares.at[d], sq_send.at[d], sq_recv.at[d], mate(d))

    each_mate(lambda d: sq_copy(d).start())

    outgoing[...] = (raw[...] + times_rows(fresh[...], rhs_at[...])).astype(jnp.bfloat16)

    def own_rows(who):
        return pl.ds(pl.multiple_of(who * SHARE, SHARE), SHARE)

    def raw_copy(d):
        return remote(
            outgoing.at[own_rows((sub + d) % GROUP)],
            incoming.at[d],
            raw_send.at[d],
            raw_recv.at[d],
            mate(d),
        )

    each_mate(lambda d: raw_copy(d).start())

    for lane in range(0, UNKNOWNS, BLOCK):
        lanes = slice(lane, lane + BLOCK)
        placed = times_rows(fresh[...], picks[lanes, :])
        blended[:, lanes] = jnp.where(
            mask[0:1, lanes] > 0.5, placed, local[:, lanes].astype(jnp.float32)
        ).astype(jnp.bfloat16)
    store_blended = pltpu.make_async_copy(blended, blended_out, store_sem.at[0])
    store_blended.start()

    each_mate(lambda d: sq_copy(d).wait_recv())
    grand = squares[0]
    for d in range(1, GROUP):
        grand += squares[d]
    factor = 1.0 / jnp.sqrt(grand / cells + 1e-05)
    for i in range(SHOTS // 128):
        scale[i * 128 : (i + 1) * 128, :] = jnp.broadcast_to(factor[i : i + 1, :], (128, 128)).T
    store_scale = pltpu.make_async_copy(scale, scale_out, store_sem.at[1])
    store_scale.start()

    each_mate(lambda d: raw_copy(d).wait_recv())
    sum_rows = outgoing[own_rows(sub), :].astype(jnp.float32)
    for d in range(1, GROUP):
        sum_rows += incoming[d].astype(jnp.float32)
    reduced[...] = (sum_rows * (scale[own_rows(sub), 0:1] / cells)).astype(jnp.bfloat16)

    def gram_copy(d):
        return remote(
            reduced,
            gram_out.at[own_rows(sub)],
            gram_send.at[d],
            gram_recv.at[d],
            mate(d),
        )

    store_gram = pltpu.make_async_copy(reduced, gram_out.at[own_rows(sub)], store_sem.at[2])
    store_gram.start()
    each_mate(lambda d: gram_copy(d).start())

    each_mate(lambda d: gram_copy(d).wait_recv())
    for side in range(2):

        @pl.when(lasting[side])
        def _():
            side_copy(side).wait_send()

    each_mate(lambda d: sq_copy(d).wait_send())
    each_mate(lambda d: raw_copy(d).wait_send())
    each_mate(lambda d: gram_copy(d).wait_send())
    store_blended.wait()
    store_scale.wait()
    store_gram.wait()


def finish(local, residual, margin_rows, blend):
    dma = pltpu.SemaphoreType.DMA
    hbm = pl.BlockSpec(memory_space=pl.ANY)
    vmem = pl.BlockSpec(memory_space=pltpu.VMEM)
    bf16 = jnp.bfloat16
    return pl.pallas_call(
        functools.partial(finish_kernel, float(GROUP * UNKNOWNS)),
        out_shape=(
            jax.ShapeDtypeStruct((SHOTS, UNKNOWNS), bf16),
            jax.ShapeDtypeStruct((SHOTS, 128), jnp.float32),
            jax.ShapeDtypeStruct((SHOTS, SHOTS), bf16),
        ),
        in_specs=[hbm, hbm, vmem, vmem],
        out_specs=(hbm, hbm, hbm),
        scratch_shapes=[
            pltpu.VMEM((SHOTS, UNKNOWNS), bf16),
            pltpu.VMEM((SHOTS, UNKNOWNS), bf16),
            pltpu.VMEM((UNKNOWNS, 2 * MARGIN), bf16),
            pltpu.VMEM((SHOTS, UNKNOWNS), bf16),
            pltpu.VMEM((2, SHOTS, MARGIN), bf16),
            pltpu.VMEM((SHOTS, 2 * MARGIN), bf16),
            pltpu.VMEM((2, SHOTS, MARGIN), bf16),
            pltpu.VMEM((SHOTS, 2 * MARGIN), bf16),
            pltpu.VMEM((SHOTS, SHOTS), jnp.float32),
            pltpu.VMEM((SHOTS, SHOTS), bf16),
            pltpu.VMEM((GROUP, SHARE, SHOTS), bf16),
            pltpu.VMEM((SHARE, SHOTS), bf16),
            pltpu.VMEM((SHOTS, UNKNOWNS), bf16),
            pltpu.VMEM((SHOTS, 128), jnp.float32),
            pltpu.VMEM((16, UNKNOWNS), jnp.float32),
            pltpu.VMEM((GROUP, 8, 128), jnp.float32),
            dma((2,)),
            dma((3,)),
            dma((2,)),
            dma((2,)),
            dma((GROUP,)),
            dma((GROUP,)),
            dma((GROUP,)),
            dma((GROUP,)),
            dma((GROUP,)),
            dma((GROUP,)),
        ],
        compiler_params=pltpu.CompilerParams(
            collective_id=1, has_side_effects=True, vmem_limit_bytes=60 * 1024 * 1024
        ),
    )(local, residual, margin_rows, blend)


def scale_kernel(blended, scale, gram_in, basis, gram):
    factor = scale[:, 0:1]
    basis[0] = (blended[...].astype(jnp.float32) * factor).astype(jnp.bfloat16)
    gram[...] = gram_in[...].astype(jnp.float32)


def scaled(blended, scale, gram):
    rows = 128

    def block(width):
        return pl.BlockSpec((rows, width), lambda i: (i, 0))

    return pl.pallas_call(
        scale_kernel,
        grid=(SHOTS // rows,),
        out_shape=(
            jax.ShapeDtypeStruct((1, SHOTS, UNKNOWNS), jnp.bfloat16),
            jax.ShapeDtypeStruct((SHOTS, SHOTS), jnp.float32),
        ),
        in_specs=[block(UNKNOWNS), block(128), block(SHOTS)],
        out_specs=(pl.BlockSpec((1, rows, UNKNOWNS), lambda i: (0, i, 0)), block(SHOTS)),
    )(blended, scale, gram)


def body(residual, lower_factor, upper_factor, margin_rows, blend):
    local = solve(residual, lower_factor, upper_factor)
    blended, scale, gram = finish(local, residual, margin_rows, blend)
    return scaled(blended, scale, gram)


def solution(mesh):
    return jax.shard_map(
        body,
        mesh=mesh,
        in_specs=(
            P("sub", "blk", None),
            P("sub", "blk", None),
            P("sub", "blk", None),
            P("sub", None, None),
            P("sub", None, None),
        ),
        out_specs=(P("sub", "blk", None), P("blk", None)),
        check_vma=False,
    )
```

```python
import functools

import jax
import jax.numpy as jnp
from jax import lax
from jax.experimental import pallas as pl
from jax.experimental.pallas import tpu as pltpu
from jax.sharding import PartitionSpec as P

MESH = pl.DeviceIdType.MESH
UNKNOWNS = 3072
SHOTS = 512
BLOCK = 384
THIRDS = 3
THIRD = BLOCK // THIRDS
BLOCKS = UNKNOWNS // BLOCK
RINGS = 4
PIECES = 4
PIECE = SHOTS // PIECES
MARGIN = 512
GROUP = 16
SHARE = SHOTS // GROUP


def times_rows(left, right):
    return lax.dot_general(
        left, right, (((1,), (1,)), ((), ())), preferred_element_type=jnp.float32
    )


def columns(k):
    return pl.ds(pl.multiple_of(k * BLOCK, BLOCK), BLOCK)


def solve_kernel(
    rhs_in,
    lower_in,
    upper_in,
    out,
    rhs,
    lower,
    upper,
    interim,
    local,
    own_sem,
    x_recv,
    x_send,
    r_recv,
    r_send,
    near_recv,
    near_send,
    far_recv,
    far_send,
    sib_recv,
    sib_send,
    ret_recv,
    ret_send,
    out_sem,
):
    sub = lax.axis_index("sub")
    blk = lax.axis_index("blk")
    core = sub % 2
    pair = sub - core
    half = blk // RINGS
    y = blk % RINGS
    guest = core != half
    home = core == half
    partner = (pair + 1 - core, (1 - half) * RINGS + y)
    sibling = (pair + 1 - core, blk)
    up = (sub, half * RINGS + (y + 1) % RINGS)
    down = (sub, half * RINGS + (y + 3) % RINGS)
    opposite = (sub, (1 - half) * RINGS + y)

    barrier = pltpu.get_barrier_semaphore()
    for other in (partner, opposite, sibling, up, down):
        pl.semaphore_signal(barrier, inc=1, device_id=other, device_id_type=MESH)
    pl.semaphore_wait(barrier, 5)

    sources = (lower_in, upper_in)
    holds = (lower, upper)
    factor = (0, 1, 1)
    ring = (core, half, 1 - half)

    def block(v, offset):
        return ring[v] * RINGS + (y + offset) % RINGS

    def span(w, b):
        return (0, b + 1) if w == 0 else (b, BLOCKS)

    def remote(src, dst, send, recv, device):
        return pltpu.make_async_remote_copy(
            src_ref=src,
            dst_ref=dst,
            send_sem=send,
            recv_sem=recv,
            device_id=device,
            device_id_type=MESH,
        )

    def whole(v, b, k):
        return holds[factor[v]].at[b, :, columns(k)]

    def part(v, b, k, p):
        return holds[factor[v]].at[b, pl.ds(p * THIRD, THIRD), columns(k)]

    def rising(v, target):
        if factor[v] == 0:
            return jnp.where(target == 2, 3, jnp.where(target == 1, 2, 1))
        return jnp.where(target == 1, 0, jnp.where(target == 2, 1, 2))

    def exchange(w, k):
        return remote(
            sources[w].at[0, :, columns(k)],
            whole(w, blk, k),
            x_send.at[w, k],
            x_recv.at[w, k],
            partner if w == 0 else opposite,
        )

    def exchange_rhs(i):
        rows = pl.ds(i * PIECE, PIECE)
        return remote(rhs_in.at[0, rows], rhs.at[rows], r_send.at[i], r_recv.at[i], partner)

    def to_near(v, k, upward, src):
        d = 0 if upward else 1
        return remote(
            src,
            whole(v, block(v, 0), k),
            near_send.at[v, d, k],
            near_recv.at[v, d, k],
            up if upward else down,
        )

    def to_far(v, b, k, p, upward):
        return remote(
            part(v, b, k, p),
            part(v, b, k, p),
            far_send.at[v, 0 if upward else 1, p, k],
            far_recv.at[v, p, k],
            up if upward else down,
        )

    def each_far(v, upward, step):
        target = (y + (1 if upward else 3)) % RINGS
        for p in range(THIRDS):

            @pl.when((p < rising(v, target)) if upward else (p >= rising(v, target)))
            def _():
                step(p)

    def to_sibling(v, b, slot, k, src):
        return remote(
            src,
            whole(v, b, k),
            sib_send.at[v, slot, k],
            sib_recv.at[v, slot, k],
            sibling,
        )

    def each(v, b, step):
        first, last = span(factor[v], b)

        def go(k, carry):
            step(k)
            return carry

        lax.fori_loop(first, last, go, 0)

    def send_own(v, k, src):
        to_near(v, k, True, src).start()
        to_near(v, k, False, src).start()
        to_sibling(v, block(v, 0), 0, k, src).start()

    def own_from_input(v):
        each(
            v,
            block(v, 0),
            lambda k: send_own(v, k, sources[factor[v]].at[0, :, columns(k)]),
        )

    def own_from_partner(v):
        def step(k):
            here = whole(v, block(v, 0), k)
            w = factor[v]
            remote(here, here, x_send.at[w, k], x_recv.at[w, k], partner).wait_recv()
            send_own(v, k, here)

        each(v, block(v, 0), step)

    def relay_from(v, upward, k):
        d = 0 if upward else 1
        b = block(v, 3 if upward else 1)
        here = whole(v, b, k)
        remote(
            here, here, near_send.at[v, d, k], near_recv.at[v, d, k], up if upward else down
        ).wait_recv()
        each_far(v, upward, lambda p: to_far(v, b, k, p, upward).start())
        to_sibling(v, b, 1 + d, k, here).start()

    def relay_near(v):
        def go(j, carry):
            for upward in (True, False):
                first, last = span(factor[v], block(v, 3 if upward else 1))

                @pl.when(first + j < last)
                def _():
                    relay_from(v, upward, first + j)

            return carry

        lax.fori_loop(0, BLOCKS, go, 0)

    def relay_across(v):
        b = block(v, 2)

        def step(k):
            for p in range(THIRDS):
                to_far(v, b, k, p, True).wait_recv()
            to_sibling(v, b, 3, k, whole(v, b, k)).start()

        each(v, b, step)

    def own_copy(w):
        return pltpu.make_async_copy(sources[w].at[0], holds[w].at[blk], own_sem.at[w])

    def rhs_copy():
        return pltpu.make_async_copy(rhs_in.at[0], rhs, own_sem.at[2])

    def turn(t):
        return jnp.where(t == 0, 0, jnp.where(t == 1, 3, t - 1))

    def from_sibling(v, b, slot):
        each(v, b, lambda k: to_sibling(v, b, slot, k, whole(v, b, k)).wait_recv())

    def lower_from_sibling(slot):
        from_sibling(0, (1 - core) * RINGS + (y + turn(slot)) % RINGS, slot)

    @pl.when(home)
    def _():
        own_from_input(0)
        rhs_copy().start()
        own_copy(0).start()
        own_copy(1).start()
        relay_near(0)
        lower_from_sibling(0)

        @pl.when(y != 1)
        def _():
            own_from_input(1)

        relay_across(0)
        lower_from_sibling(1)
        lower_from_sibling(2)

        @pl.when(y == 1)
        def _():
            own_from_input(1)

        own_from_partner(2)
        relay_near(1)
        rhs_copy().wait()
        own_copy(0).wait()
        own_copy(1).wait()

    @pl.when(guest)
    def _():
        each(0, blk, lambda k: exchange(0, k).start())

        @pl.when(half == 0)
        def _():
            each(1, blk, lambda k: exchange(1, k).start())

        own_from_partner(0)
        for i in range(PIECES):
            exchange_rhs(i).start()

        @pl.when(half == 1)
        def _():
            each(1, blk, lambda k: exchange(1, k).start())

        relay_near(0)
        relay_across(0)
        for i in range(PIECES):
            exchange_rhs(i).wait_recv()
        lower_from_sibling(0)
        lower_from_sibling(1)
        lower_from_sibling(2)

    lower_from_sibling(3)

    for b in range(BLOCKS):
        stop = (b + 1) * BLOCK
        interim[:, b * BLOCK : stop] = (
            times_rows(lower[b, :, :stop], rhs[:, :stop]).astype(jnp.bfloat16).T
        )

    @pl.when(home)
    def _():
        relay_near(2)
        relay_across(1)

    def back(b):
        return remote(
            local.at[:, columns(b)],
            out.at[:, columns(b)],
            ret_send.at[b],
            ret_recv.at[b],
            partner,
        )

    def keep(b):
        return pltpu.make_async_copy(
            local.at[:, columns(b)], out.at[:, columns(b)], out_sem.at[b]
        )

    def solve_step(t, carry):
        first_half = (t == 0) | (t == 2) | (t == 3) | (t == 6)
        slot = jnp.where(t < 2, 0, jnp.where(t > 5, 3, 1 + t % 2))
        this = jnp.where(first_half, half, 1 - half) * RINGS + (y + turn(slot)) % RINGS

        @pl.when(home & (t == 6))
        def _():
            relay_across(2)

        @pl.when(guest & first_half)
        def _():
            from_sibling(1, this, slot)

        @pl.when(guest & jnp.logical_not(first_half))
        def _():
            from_sibling(2, this, slot)

        for b in range(BLOCKS):

            @pl.when(this == b)
            def _():
                start = b * BLOCK
                local[:, start : start + BLOCK] = (
                    times_rows(upper[b, :, start:], interim[:, start:]).astype(jnp.bfloat16).T
                )

        @pl.when(guest)
        def _():
            back(this).start()

        @pl.when(home)
        def _():
            keep(this).start()

        return carry

    lax.fori_loop(0, BLOCKS, solve_step, 0)

    def sent(v):
        def own_sent(k):
            here = whole(v, block(v, 0), k)
            to_near(v, k, True, here).wait_send()
            to_near(v, k, False, here).wait_send()
            to_sibling(v, block(v, 0), 0, k, here).wait_send()

        each(v, block(v, 0), own_sent)
        for upward in (True, False):
            b = block(v, 3 if upward else 1)

            def near_sent(k):
                each_far(v, upward, lambda p: to_far(v, b, k, p, upward).wait_send())
                to_sibling(v, b, 1 if upward else 2, k, whole(v, b, k)).wait_send()

            each(v, b, near_sent)
        b = block(v, 2)
        each(v, b, lambda k: to_sibling(v, b, 3, k, whole(v, b, k)).wait_send())

    sent(0)

    @pl.when(home)
    def _():
        sent(1)
        sent(2)

    @pl.when(guest)
    def _():
        for w in range(2):
            each(w, blk, lambda k: exchange(w, k).wait_send())
        for i in range(PIECES):
            exchange_rhs(i).wait_send()

    def finish(b, carry):
        @pl.when(guest)
        def _():
            back(b).wait()

        @pl.when(home)
        def _():
            keep(b).wait()

        return carry

    lax.fori_loop(0, BLOCKS, finish, 0)


def solve(residual, lower_factor, upper_factor):
    dma = pltpu.SemaphoreType.DMA
    hbm = pl.BlockSpec(memory_space=pl.ANY)
    return pl.pallas_call(
        solve_kernel,
        out_shape=jax.ShapeDtypeStruct((SHOTS, UNKNOWNS), jnp.bfloat16),
        in_specs=[hbm] * 3,
        out_specs=hbm,
        scratch_shapes=[
            pltpu.VMEM((SHOTS, UNKNOWNS), jnp.bfloat16),
            pltpu.VMEM((BLOCKS, BLOCK, UNKNOWNS), jnp.bfloat16),
            pltpu.VMEM((BLOCKS, BLOCK, UNKNOWNS), jnp.bfloat16),
            pltpu.VMEM((SHOTS, UNKNOWNS), jnp.bfloat16),
            pltpu.VMEM((SHOTS, UNKNOWNS), jnp.bfloat16),
            dma((3,)),
            dma((2, BLOCKS)),
            dma((2, BLOCKS)),
            dma((PIECES,)),
            dma((PIECES,)),
            dma((3, 2, BLOCKS)),
            dma((3, 2, BLOCKS)),
            dma((3, THIRDS, BLOCKS)),
            dma((3, 2, THIRDS, BLOCKS)),
            dma((3, RINGS, BLOCKS)),
            dma((3, RINGS, BLOCKS)),
            dma((BLOCKS,)),
            dma((BLOCKS,)),
            dma((BLOCKS,)),
        ],
        compiler_params=pltpu.CompilerParams(
            collective_id=0, has_side_effects=True, vmem_limit_bytes=60 * 1024 * 1024
        ),
        cost_estimate=pl.CostEstimate(
            flops=2 * 36 * 2 * SHOTS * BLOCK * BLOCK,
            bytes_accessed=5 * SHOTS * UNKNOWNS * 2,
            transcendentals=0,
        ),
    )(residual, lower_factor, upper_factor)


def finish_kernel(
    cells,
    local_in,
    rhs_in,
    rows_in,
    blend_in,
    blended_out,
    scale_out,
    gram_out,
    local,
    rhs,
    picks,
    kept,
    at,
    fresh,
    neighbour,
    rhs_at,
    raw,
    outgoing,
    incoming,
    reduced,
    blended,
    scale,
    mask,
    squares,
    load_sem,
    store_sem,
    side_send,
    side_recv,
    sq_send,
    sq_recv,
    raw_send,
    raw_recv,
    gram_send,
    gram_recv,
):
    sub = lax.axis_index("sub")
    blk = lax.axis_index("blk")

    def mate(d):
        return ((sub + d) % GROUP, blk)

    def remote(src, dst, send, recv, device):
        return pltpu.make_async_remote_copy(
            src_ref=src,
            dst_ref=dst,
            send_sem=send,
            recv_sem=recv,
            device_id=device,
            device_id_type=MESH,
        )

    def each_mate(step):
        def go(d, carry):
            step(d)
            return carry

        lax.fori_loop(1, GROUP, go, 0)

    barrier = pltpu.get_barrier_semaphore()
    each_mate(
        lambda d: pl.semaphore_signal(barrier, inc=1, device_id=mate(d), device_id_type=MESH)
    )
    load_local = pltpu.make_async_copy(local_in, local, load_sem.at[0])
    load_rhs = pltpu.make_async_copy(rhs_in.at[0], rhs, load_sem.at[1])
    load_local.start()
    load_rhs.start()

    def pick(i, carry):
        place = pl.ds(pl.multiple_of(i * 256, 256), 256)
        unknown = lax.broadcasted_iota(jnp.int32, (256, MARGIN), 0) + i * 256
        for side in range(2):
            hit = unknown == rows_in[0, side : side + 1, :]
            picks[place, side * MARGIN : (side + 1) * MARGIN] = jnp.where(
                hit, jnp.float32(1), jnp.float32(0)
            ).astype(jnp.bfloat16)
        return carry

    lax.fori_loop(0, UNKNOWNS // 256, pick, 0)
    load_local.wait()
    pl.semaphore_wait(barrier, GROUP - 1)

    def picked(values):
        return lambda lanes: jnp.dot(
            values[...], picks[:, lanes], preferred_element_type=jnp.float32
        ).astype(jnp.bfloat16)

    def side_copy(side, i):
        lanes = pl.ds(i * 256, 256)
        return remote(
            at.at[side, :, lanes],
            neighbour.at[1 - side, :, lanes],
            side_send.at[side, i],
            side_recv.at[1 - side, i],
            ((sub + (GROUP - 1 if side == 0 else 1)) % GROUP, blk),
        )

    lasting = (sub > 0, sub < GROUP - 1)

    at_side = picked(local)
    for i in range(MARGIN // 256):
        for side in range(2):
            lanes = side * MARGIN + i * 256
            at[side, :, i * 256 : (i + 1) * 256] = at_side(slice(lanes, lanes + 256))

            @pl.when(lasting[side])
            def _():
                side_copy(side, i).start()

    mask[...] = times_rows(jnp.ones((16, 2 * MARGIN), jnp.bfloat16), picks[...])

    def keep_rows(i, carry):
        place = pl.ds(pl.multiple_of(i * 64, 64), 64)
        rest = jnp.where(mask[0:1, :] > 0.5, 0.0, local[place, :].astype(jnp.float32))
        kept[place, :] = rest.astype(jnp.bfloat16)
        total = jnp.zeros((64, 128), jnp.float32)
        for lane in range(0, UNKNOWNS, 128):
            piece = rest[:, lane : lane + 128]
            total += piece * piece
        scale[place, :] = total
        return carry

    lax.fori_loop(0, SHOTS // 64, keep_rows, 0)
    load_rhs.wait()
    at_rhs = picked(rhs)
    for lanes in range(0, 2 * MARGIN, 256):
        rhs_at[:, lanes : lanes + 256] = at_rhs(slice(lanes, lanes + 256))
    for lanes in range(0, SHOTS, 256):
        raw[:, lanes : lanes + 256] = times_rows(kept[...], rhs[lanes : lanes + 256, :])

    for side in range(2):
        lanes = slice(side * MARGIN, (side + 1) * MARGIN)

        @pl.when(lasting[side])
        def _():
            for i in range(MARGIN // 256):
                side_copy(1 - side, i).wait_recv()
            value = at[side].astype(jnp.float32)
            other = neighbour[side].astype(jnp.float32)
            fresh[:, lanes] = (
                value + blend_in[0, side : side + 1, :] * (other - value)
            ).astype(jnp.bfloat16)

        @pl.when(jnp.logical_not(lasting[side]))
        def _():
            fresh[:, lanes] = at[side]

    total = scale[...]
    for lane in range(0, 2 * MARGIN, 128):
        piece = fresh[:, lane : lane + 128].astype(jnp.float32)
        total += piece * piece
    across = jnp.sum(total.T, axis=0, keepdims=True)
    squares[0] = jnp.zeros((8, 128), jnp.float32)
    for i in range(SHOTS // 128):
        squares[0, i : i + 1, :] = across[:, i * 128 : (i + 1) * 128]

    def sq_copy(d):
        return remote(squares.at[0], squares.at[d], sq_send.at[d], sq_recv.at[d], mate(d))

    each_mate(lambda d: sq_copy(d).start())

    outgoing[...] = (raw[...] + times_rows(fresh[...], rhs_at[...])).astype(jnp.bfloat16)

    def own_rows(who):
        return pl.ds(pl.multiple_of(who * SHARE, SHARE), SHARE)

    def raw_copy(d):
        return remote(
            outgoing.at[own_rows((sub + d) % GROUP)],
            incoming.at[d],
            raw_send.at[d],
            raw_recv.at[d],
            mate(d),
        )

    each_mate(lambda d: raw_copy(d).start())

    for lane in range(0, UNKNOWNS, BLOCK):
        lanes = slice(lane, lane + BLOCK)
        placed = times_rows(fresh[...], picks[lanes, :])
        blended[:, lanes] = jnp.where(
            mask[0:1, lanes] > 0.5, placed, local[:, lanes].astype(jnp.float32)
        ).astype(jnp.bfloat16)
    store_blended = pltpu.make_async_copy(blended, blended_out, store_sem.at[0])
    store_blended.start()

    each_mate(lambda d: sq_copy(d).wait_recv())
    grand = squares[0]
    for d in range(1, GROUP):
        grand += squares[d]
    factor = 1.0 / jnp.sqrt(grand / cells + 1e-05)
    for i in range(SHOTS // 128):
        scale[i * 128 : (i + 1) * 128, :] = jnp.broadcast_to(factor[i : i + 1, :], (128, 128)).T
    store_scale = pltpu.make_async_copy(scale, scale_out, store_sem.at[1])
    store_scale.start()

    each_mate(lambda d: raw_copy(d).wait_recv())
    sum_rows = outgoing[own_rows(sub), :].astype(jnp.float32)
    for d in range(1, GROUP):
        sum_rows += incoming[d].astype(jnp.float32)
    reduced[...] = (sum_rows * (scale[own_rows(sub), 0:1] / cells)).astype(jnp.bfloat16)

    def gram_copy(d):
        return remote(
            reduced,
            gram_out.at[own_rows(sub)],
            gram_send.at[d],
            gram_recv.at[d],
            mate(d),
        )

    store_gram = pltpu.make_async_copy(reduced, gram_out.at[own_rows(sub)], store_sem.at[2])
    store_gram.start()
    each_mate(lambda d: gram_copy(d).start())

    each_mate(lambda d: gram_copy(d).wait_recv())
    for side in range(2):

        @pl.when(lasting[side])
        def _():
            for i in range(MARGIN // 256):
                side_copy(side, i).wait_send()

    each_mate(lambda d: sq_copy(d).wait_send())
    each_mate(lambda d: raw_copy(d).wait_send())
    each_mate(lambda d: gram_copy(d).wait_send())
    store_blended.wait()
    store_scale.wait()
    store_gram.wait()


def finish(local, residual, margin_rows, blend):
    dma = pltpu.SemaphoreType.DMA
    hbm = pl.BlockSpec(memory_space=pl.ANY)
    vmem = pl.BlockSpec(memory_space=pltpu.VMEM)
    bf16 = jnp.bfloat16
    return pl.pallas_call(
        functools.partial(finish_kernel, float(GROUP * UNKNOWNS)),
        out_shape=(
            jax.ShapeDtypeStruct((SHOTS, UNKNOWNS), bf16),
            jax.ShapeDtypeStruct((SHOTS, 128), jnp.float32),
            jax.ShapeDtypeStruct((SHOTS, SHOTS), bf16),
        ),
        in_specs=[hbm, hbm, vmem, vmem],
        out_specs=(hbm, hbm, hbm),
        scratch_shapes=[
            pltpu.VMEM((SHOTS, UNKNOWNS), bf16),
            pltpu.VMEM((SHOTS, UNKNOWNS), bf16),
            pltpu.VMEM((UNKNOWNS, 2 * MARGIN), bf16),
            pltpu.VMEM((SHOTS, UNKNOWNS), bf16),
            pltpu.VMEM((2, SHOTS, MARGIN), bf16),
            pltpu.VMEM((SHOTS, 2 * MARGIN), bf16),
            pltpu.VMEM((2, SHOTS, MARGIN), bf16),
            pltpu.VMEM((SHOTS, 2 * MARGIN), bf16),
            pltpu.VMEM((SHOTS, SHOTS), jnp.float32),
            pltpu.VMEM((SHOTS, SHOTS), bf16),
            pltpu.VMEM((GROUP, SHARE, SHOTS), bf16),
            pltpu.VMEM((SHARE, SHOTS), bf16),
            pltpu.VMEM((SHOTS, UNKNOWNS), bf16),
            pltpu.VMEM((SHOTS, 128), jnp.float32),
            pltpu.VMEM((16, UNKNOWNS), jnp.float32),
            pltpu.VMEM((GROUP, 8, 128), jnp.float32),
            dma((2,)),
            dma((3,)),
            dma((2, MARGIN // 256)),
            dma((2, MARGIN // 256)),
            dma((GROUP,)),
            dma((GROUP,)),
            dma((GROUP,)),
            dma((GROUP,)),
            dma((GROUP,)),
            dma((GROUP,)),
        ],
        compiler_params=pltpu.CompilerParams(
            collective_id=1, has_side_effects=True, vmem_limit_bytes=60 * 1024 * 1024
        ),
    )(local, residual, margin_rows, blend)


def scale_kernel(blended, scale, gram_in, basis, gram):
    factor = scale[:, 0:1]
    basis[0] = (blended[...].astype(jnp.float32) * factor).astype(jnp.bfloat16)
    gram[...] = gram_in[...].astype(jnp.float32)


def scaled(blended, scale, gram):
    rows = 256

    def block(width):
        return pl.BlockSpec((rows, width), lambda i: (i, 0))

    return pl.pallas_call(
        scale_kernel,
        grid=(SHOTS // rows,),
        out_shape=(
            jax.ShapeDtypeStruct((1, SHOTS, UNKNOWNS), jnp.bfloat16),
            jax.ShapeDtypeStruct((SHOTS, SHOTS), jnp.float32),
        ),
        in_specs=[block(UNKNOWNS), block(128), block(SHOTS)],
        out_specs=(pl.BlockSpec((1, rows, UNKNOWNS), lambda i: (0, i, 0)), block(SHOTS)),
    )(blended, scale, gram)


def body(residual, lower_factor, upper_factor, margin_rows, blend):
    local = solve(residual, lower_factor, upper_factor)
    blended, scale, gram = finish(local, residual, margin_rows, blend)
    return scaled(blended, scale, gram)


def solution(mesh):
    return jax.shard_map(
        body,
        mesh=mesh,
        in_specs=(
            P("sub", "blk", None),
            P("sub", "blk", None),
            P("sub", "blk", None),
            P("sub", None, None),
            P("sub", None, None),
        ),
        out_specs=(P("sub", "blk", None), P("blk", None)),
        check_vma=False,
    )
```

```python
import functools

import jax
import jax.numpy as jnp
from jax import lax
from jax.experimental import pallas as pl
from jax.experimental.pallas import tpu as pltpu
from jax.sharding import PartitionSpec as P

MESH = pl.DeviceIdType.MESH
UNKNOWNS = 3072
SHOTS = 512
BLOCK = 384
THIRDS = 3
PICKED = UNKNOWNS // 16
THIRD = BLOCK // THIRDS
BLOCKS = UNKNOWNS // BLOCK
RINGS = 4
PIECES = 4
PIECE = SHOTS // PIECES
MARGIN = 512
GROUP = 16
SHARE = SHOTS // GROUP


def times_rows(left, right):
    return lax.dot_general(
        left, right, (((1,), (1,)), ((), ())), preferred_element_type=jnp.float32
    )


def columns(k):
    return pl.ds(pl.multiple_of(k * BLOCK, BLOCK), BLOCK)


def apply_kernel(
    cells,
    rhs_in,
    lower_in,
    upper_in,
    rows_in,
    blend_in,
    blended_out,
    scale_out,
    gram_out,
    rhs,
    lower,
    upper,
    interim,
    local,
    final,
    picks,
    at,
    fresh,
    neighbour,
    rhs_at,
    raw,
    outgoing,
    incoming,
    reduced,
    scale,
    mask,
    squares,
    own_sem,
    x_recv,
    x_send,
    r_recv,
    r_send,
    near_recv,
    near_send,
    far_recv,
    far_send,
    sib_recv,
    sib_send,
    ret_recv,
    ret_send,
    out_sem,
    store_sem,
    side_send,
    side_recv,
    sq_send,
    sq_recv,
    raw_send,
    raw_recv,
    gram_send,
    gram_recv,
):
    sub = lax.axis_index("sub")
    blk = lax.axis_index("blk")
    core = sub % 2
    pair = sub - core
    half = blk // RINGS
    y = blk % RINGS
    guest = core != half
    home = core == half
    partner = (pair + 1 - core, (1 - half) * RINGS + y)
    sibling = (pair + 1 - core, blk)
    up = (sub, half * RINGS + (y + 1) % RINGS)
    down = (sub, half * RINGS + (y + 3) % RINGS)
    opposite = (sub, (1 - half) * RINGS + y)

    def mate(d):
        return ((sub + d) % GROUP, blk)

    def each_mate(step):
        def go(d, carry):
            step(d)
            return carry

        lax.fori_loop(1, GROUP, go, 0)

    barrier = pltpu.get_barrier_semaphore()
    for other in (partner, opposite, up, down):
        pl.semaphore_signal(barrier, inc=1, device_id=other, device_id_type=MESH)
    each_mate(
        lambda d: pl.semaphore_signal(barrier, inc=1, device_id=mate(d), device_id_type=MESH)
    )
    pl.semaphore_wait(barrier, 4 + GROUP - 1)

    sources = (lower_in, upper_in)
    holds = (lower, upper)
    factor = (0, 1, 1)
    ring = (core, half, 1 - half)

    def block(v, offset):
        return ring[v] * RINGS + (y + offset) % RINGS

    def span(w, b):
        return (0, b + 1) if w == 0 else (b, BLOCKS)

    def remote(src, dst, send, recv, device):
        return pltpu.make_async_remote_copy(
            src_ref=src,
            dst_ref=dst,
            send_sem=send,
            recv_sem=recv,
            device_id=device,
            device_id_type=MESH,
        )

    def whole(v, b, k):
        return holds[factor[v]].at[b, :, columns(k)]

    def part(v, b, k, p):
        return holds[factor[v]].at[b, pl.ds(p * THIRD, THIRD), columns(k)]

    def rising(v, target):
        if factor[v] == 0:
            return jnp.where(target == 2, 3, jnp.where(target == 1, 2, 1))
        return jnp.where(target == 1, 0, jnp.where(target == 2, 1, 2))

    def exchange(w, k):
        return remote(
            sources[w].at[0, :, columns(k)],
            whole(w, blk, k),
            x_send.at[w, k],
            x_recv.at[w, k],
            partner if w == 0 else opposite,
        )

    def exchange_rhs(i):
        rows = pl.ds(i * PIECE, PIECE)
        return remote(rhs_in.at[0, rows], rhs.at[rows], r_send.at[i], r_recv.at[i], partner)

    def to_near(v, k, upward, src):
        d = 0 if upward else 1
        return remote(
            src,
            whole(v, block(v, 0), k),
            near_send.at[v, d, k],
            near_recv.at[v, d, k],
            up if upward else down,
        )

    def to_far(v, b, k, p, upward):
        return remote(
            part(v, b, k, p),
            part(v, b, k, p),
            far_send.at[v, 0 if upward else 1, p, k],
            far_recv.at[v, p, k],
            up if upward else down,
        )

    def each_far(v, upward, step):
        target = (y + (1 if upward else 3)) % RINGS
        for p in range(THIRDS):

            @pl.when((p < rising(v, target)) if upward else (p >= rising(v, target)))
            def _():
                step(p)

    def to_sibling(v, b, slot, k, src):
        return remote(
            src,
            whole(v, b, k),
            sib_send.at[v, slot, k],
            sib_recv.at[v, slot, k],
            sibling,
        )

    def each(v, b, step):
        first, last = span(factor[v], b)

        def go(k, carry):
            step(k)
            return carry

        lax.fori_loop(first, last, go, 0)

    def send_own(v, k, src):
        to_near(v, k, True, src).start()
        to_near(v, k, False, src).start()
        to_sibling(v, block(v, 0), 0, k, src).start()

    def own_from_input(v):
        each(
            v,
            block(v, 0),
            lambda k: send_own(v, k, sources[factor[v]].at[0, :, columns(k)]),
        )

    def own_from_partner(v):
        def step(k):
            here = whole(v, block(v, 0), k)
            w = factor[v]
            remote(here, here, x_send.at[w, k], x_recv.at[w, k], partner).wait_recv()
            send_own(v, k, here)

        each(v, block(v, 0), step)

    def relay_from(v, upward, k):
        d = 0 if upward else 1
        b = block(v, 3 if upward else 1)
        here = whole(v, b, k)
        remote(
            here, here, near_send.at[v, d, k], near_recv.at[v, d, k], up if upward else down
        ).wait_recv()
        each_far(v, upward, lambda p: to_far(v, b, k, p, upward).start())
        to_sibling(v, b, 1 + d, k, here).start()

    def pick(i):
        place = pl.ds(pl.multiple_of(i * PICKED, PICKED), PICKED)
        unknown = lax.broadcasted_iota(jnp.int32, (PICKED, MARGIN), 0) + i * PICKED
        for side in range(2):
            hit = unknown == rows_in[0, side : side + 1, :]
            picks[place, side * MARGIN : (side + 1) * MARGIN] = jnp.where(
                hit, jnp.float32(1), jnp.float32(0)
            ).astype(jnp.bfloat16)

    def relay_near(v):
        def go(j, carry):
            if v == 0:
                pick(2 * j)
                pick(2 * j + 1)
            for upward in (True, False):
                first, last = span(factor[v], block(v, 3 if upward else 1))

                @pl.when(first + j < last)
                def _():
                    relay_from(v, upward, first + j)

            return carry

        lax.fori_loop(0, BLOCKS, go, 0)

    def relay_across(v):
        b = block(v, 2)

        def step(k):
            for p in range(THIRDS):
                to_far(v, b, k, p, True).wait_recv()
            to_sibling(v, b, 3, k, whole(v, b, k)).start()

        each(v, b, step)

    def own_copy(w):
        return pltpu.make_async_copy(sources[w].at[0], holds[w].at[blk], own_sem.at[w])

    def rhs_copy():
        return pltpu.make_async_copy(rhs_in.at[0], rhs, own_sem.at[2])

    def turn(t):
        return jnp.where(t == 0, 0, jnp.where(t == 1, 3, t - 1))

    def from_sibling(v, b, slot):
        each(v, b, lambda k: to_sibling(v, b, slot, k, whole(v, b, k)).wait_recv())

    def lower_from_sibling(slot):
        from_sibling(0, (1 - core) * RINGS + (y + turn(slot)) % RINGS, slot)

    @pl.when(home)
    def _():
        own_from_input(0)
        rhs_copy().start()
        own_copy(0).start()
        own_copy(1).start()

    @pl.when(guest)
    def _():
        each(0, blk, lambda k: exchange(0, k).start())

        @pl.when(half == 0)
        def _():
            each(1, blk, lambda k: exchange(1, k).start())

    @pl.when(home)
    def _():
        relay_near(0)
        lower_from_sibling(0)

        @pl.when(y != 1)
        def _():
            own_from_input(1)

        relay_across(0)
        lower_from_sibling(1)
        lower_from_sibling(2)

        @pl.when(y == 1)
        def _():
            own_from_input(1)

        own_from_partner(2)
        relay_near(1)
        rhs_copy().wait()
        own_copy(0).wait()
        own_copy(1).wait()

    @pl.when(guest)
    def _():
        own_from_partner(0)
        for i in range(PIECES):
            exchange_rhs(i).start()

        @pl.when(half == 1)
        def _():
            each(1, blk, lambda k: exchange(1, k).start())

        relay_near(0)
        relay_across(0)
        for i in range(PIECES):
            exchange_rhs(i).wait_recv()
        lower_from_sibling(0)
        lower_from_sibling(1)
        lower_from_sibling(2)

    lower_from_sibling(3)

    for b in range(BLOCKS):
        stop = (b + 1) * BLOCK
        interim[:, b * BLOCK : stop] = (
            times_rows(lower[b, :, :stop], rhs[:, :stop]).astype(jnp.bfloat16).T
        )

    @pl.when(guest)
    def _():
        rhs_copy().start()

    @pl.when(home)
    def _():
        relay_near(2)
        relay_across(1)

    def back(b):
        return remote(
            local.at[:, columns(b)],
            final.at[:, columns(b)],
            ret_send.at[b],
            ret_recv.at[b],
            partner,
        )

    def keep(b):
        return pltpu.make_async_copy(
            local.at[:, columns(b)], final.at[:, columns(b)], out_sem.at[b]
        )

    def solve_step(t, carry):
        first_half = (t == 0) | (t == 2) | (t == 3) | (t == 6)
        slot = jnp.where(t < 2, 0, jnp.where(t > 5, 3, 1 + t % 2))
        this = jnp.where(first_half, half, 1 - half) * RINGS + (y + turn(slot)) % RINGS

        @pl.when(home & (t == 6))
        def _():
            relay_across(2)

        @pl.when(guest & first_half)
        def _():
            from_sibling(1, this, slot)

        @pl.when(guest & jnp.logical_not(first_half))
        def _():
            from_sibling(2, this, slot)

        for b in range(BLOCKS):

            @pl.when(this == b)
            def _():
                start = b * BLOCK
                local[:, start : start + BLOCK] = (
                    times_rows(upper[b, :, start:], interim[:, start:]).astype(jnp.bfloat16).T
                )

        @pl.when(guest)
        def _():
            back(this).start()

        @pl.when(home)
        def _():
            keep(this).start()

        return carry

    lax.fori_loop(0, BLOCKS, solve_step, 0)

    @pl.when(guest)
    def _():
        rhs_copy().wait()

    def picked(values):
        return lambda lanes: jnp.dot(
            values[...], picks[:, lanes], preferred_element_type=jnp.float32
        ).astype(jnp.bfloat16)

    mask[...] = times_rows(jnp.ones((16, 2 * MARGIN), jnp.bfloat16), picks[...])
    at_rhs = picked(rhs)
    for lanes in range(0, 2 * MARGIN, 256):
        rhs_at[:, lanes : lanes + 256] = at_rhs(slice(lanes, lanes + 256))

    def sent(v):
        def own_sent(k):
            here = whole(v, block(v, 0), k)
            to_near(v, k, True, here).wait_send()
            to_near(v, k, False, here).wait_send()
            to_sibling(v, block(v, 0), 0, k, here).wait_send()

        each(v, block(v, 0), own_sent)
        for upward in (True, False):
            b = block(v, 3 if upward else 1)

            def near_sent(k):
                each_far(v, upward, lambda p: to_far(v, b, k, p, upward).wait_send())
                to_sibling(v, b, 1 if upward else 2, k, whole(v, b, k)).wait_send()

            each(v, b, near_sent)
        b = block(v, 2)
        each(v, b, lambda k: to_sibling(v, b, 3, k, whole(v, b, k)).wait_send())

    sent(0)

    @pl.when(home)
    def _():
        sent(1)
        sent(2)

    @pl.when(guest)
    def _():
        for w in range(2):
            each(w, blk, lambda k: exchange(w, k).wait_send())
        for i in range(PIECES):
            exchange_rhs(i).wait_send()

    def finish(b, carry):
        @pl.when(guest)
        def _():
            back(b).wait()

        @pl.when(home)
        def _():
            keep(b).wait()

        return carry

    lax.fori_loop(0, BLOCKS, finish, 0)

    def side_copy(side, i):
        lanes = pl.ds(i * 256, 256)
        return remote(
            at.at[side, :, lanes],
            neighbour.at[1 - side, :, lanes],
            side_send.at[side, i],
            side_recv.at[1 - side, i],
            ((sub + (GROUP - 1 if side == 0 else 1)) % GROUP, blk),
        )

    lasting = (sub > 0, sub < GROUP - 1)

    at_side = picked(final)
    for i in range(MARGIN // 256):
        for side in range(2):
            lanes = side * MARGIN + i * 256
            at[side, :, i * 256 : (i + 1) * 256] = at_side(slice(lanes, lanes + 256))

            @pl.when(lasting[side])
            def _():
                side_copy(side, i).start()

    def keep_rows(i, carry):
        place = pl.ds(pl.multiple_of(i * 64, 64), 64)
        rest = jnp.where(mask[0:1, :] > 0.5, 0.0, final[place, :].astype(jnp.float32))
        interim[place, :] = rest.astype(jnp.bfloat16)
        total = jnp.zeros((64, 128), jnp.float32)
        for lane in range(0, UNKNOWNS, 128):
            piece = rest[:, lane : lane + 128]
            total += piece * piece
        scale[place, :] = total
        return carry

    lax.fori_loop(0, SHOTS // 64, keep_rows, 0)
    for lanes in range(0, SHOTS, 256):
        raw[:, lanes : lanes + 256] = times_rows(interim[...], rhs[lanes : lanes + 256, :])

    for side in range(2):
        lanes = slice(side * MARGIN, (side + 1) * MARGIN)

        @pl.when(lasting[side])
        def _():
            for i in range(MARGIN // 256):
                side_copy(1 - side, i).wait_recv()
            value = at[side].astype(jnp.float32)
            other = neighbour[side].astype(jnp.float32)
            fresh[:, lanes] = (
                value + blend_in[0, side : side + 1, :] * (other - value)
            ).astype(jnp.bfloat16)

        @pl.when(jnp.logical_not(lasting[side]))
        def _():
            fresh[:, lanes] = at[side]

    total = scale[...]
    for lane in range(0, 2 * MARGIN, 128):
        piece = fresh[:, lane : lane + 128].astype(jnp.float32)
        total += piece * piece
    across = jnp.sum(total.T, axis=0, keepdims=True)
    squares[0] = jnp.zeros((8, 128), jnp.float32)
    for i in range(SHOTS // 128):
        squares[0, i : i + 1, :] = across[:, i * 128 : (i + 1) * 128]

    def sq_copy(d):
        return remote(squares.at[0], squares.at[d], sq_send.at[d], sq_recv.at[d], mate(d))

    each_mate(lambda d: sq_copy(d).start())

    outgoing[...] = (raw[...] + times_rows(fresh[...], rhs_at[...])).astype(jnp.bfloat16)

    def own_rows(who):
        return pl.ds(pl.multiple_of(who * SHARE, SHARE), SHARE)

    def raw_copy(d):
        return remote(
            outgoing.at[own_rows((sub + d) % GROUP)],
            incoming.at[d],
            raw_send.at[d],
            raw_recv.at[d],
            mate(d),
        )

    each_mate(lambda d: raw_copy(d).start())

    for lane in range(0, UNKNOWNS, BLOCK):
        lanes = slice(lane, lane + BLOCK)
        placed = times_rows(fresh[...], picks[lanes, :])
        local[:, lanes] = jnp.where(
            mask[0:1, lanes] > 0.5, placed, final[:, lanes].astype(jnp.float32)
        ).astype(jnp.bfloat16)
    store_blended = pltpu.make_async_copy(local, blended_out, store_sem.at[0])
    store_blended.start()

    each_mate(lambda d: sq_copy(d).wait_recv())
    grand = squares[0]
    for d in range(1, GROUP):
        grand += squares[d]
    factor = 1.0 / jnp.sqrt(grand / cells + 1e-05)
    for i in range(SHOTS // 128):
        scale[i * 128 : (i + 1) * 128, :] = jnp.broadcast_to(factor[i : i + 1, :], (128, 128)).T
    store_scale = pltpu.make_async_copy(scale, scale_out, store_sem.at[1])
    store_scale.start()

    each_mate(lambda d: raw_copy(d).wait_recv())
    sum_rows = outgoing[own_rows(sub), :].astype(jnp.float32)
    for d in range(1, GROUP):
        sum_rows += incoming[d].astype(jnp.float32)
    reduced[...] = (sum_rows * (scale[own_rows(sub), 0:1] / cells)).astype(jnp.bfloat16)

    def gram_copy(d):
        return remote(
            reduced,
            gram_out.at[own_rows(sub)],
            gram_send.at[d],
            gram_recv.at[d],
            mate(d),
        )

    store_gram = pltpu.make_async_copy(reduced, gram_out.at[own_rows(sub)], store_sem.at[2])
    store_gram.start()
    each_mate(lambda d: gram_copy(d).start())

    each_mate(lambda d: gram_copy(d).wait_recv())
    for side in range(2):

        @pl.when(lasting[side])
        def _():
            for i in range(MARGIN // 256):
                side_copy(side, i).wait_send()

    each_mate(lambda d: sq_copy(d).wait_send())
    each_mate(lambda d: raw_copy(d).wait_send())
    each_mate(lambda d: gram_copy(d).wait_send())
    store_blended.wait()
    store_scale.wait()
    store_gram.wait()


def apply(residual, lower_factor, upper_factor, margin_rows, blend):
    dma = pltpu.SemaphoreType.DMA
    hbm = pl.BlockSpec(memory_space=pl.ANY)
    vmem = pl.BlockSpec(memory_space=pltpu.VMEM)
    bf16 = jnp.bfloat16
    return pl.pallas_call(
        functools.partial(apply_kernel, float(GROUP * UNKNOWNS)),
        out_shape=(
            jax.ShapeDtypeStruct((SHOTS, UNKNOWNS), bf16),
            jax.ShapeDtypeStruct((SHOTS, 128), jnp.float32),
            jax.ShapeDtypeStruct((SHOTS, SHOTS), bf16),
        ),
        in_specs=[hbm, hbm, hbm, vmem, vmem],
        out_specs=(hbm, hbm, hbm),
        scratch_shapes=[
            pltpu.VMEM((SHOTS, UNKNOWNS), bf16),
            pltpu.VMEM((BLOCKS, BLOCK, UNKNOWNS), bf16),
            pltpu.VMEM((BLOCKS, BLOCK, UNKNOWNS), bf16),
            pltpu.VMEM((SHOTS, UNKNOWNS), bf16),
            pltpu.VMEM((SHOTS, UNKNOWNS), bf16),
            pltpu.VMEM((SHOTS, UNKNOWNS), bf16),
            pltpu.VMEM((UNKNOWNS, 2 * MARGIN), bf16),
            pltpu.VMEM((2, SHOTS, MARGIN), bf16),
            pltpu.VMEM((SHOTS, 2 * MARGIN), bf16),
            pltpu.VMEM((2, SHOTS, MARGIN), bf16),
            pltpu.VMEM((SHOTS, 2 * MARGIN), bf16),
            pltpu.VMEM((SHOTS, SHOTS), jnp.float32),
            pltpu.VMEM((SHOTS, SHOTS), bf16),
            pltpu.VMEM((GROUP, SHARE, SHOTS), bf16),
            pltpu.VMEM((SHARE, SHOTS), bf16),
            pltpu.VMEM((SHOTS, 128), jnp.float32),
            pltpu.VMEM((16, UNKNOWNS), jnp.float32),
            pltpu.VMEM((GROUP, 8, 128), jnp.float32),
            dma((3,)),
            dma((2, BLOCKS)),
            dma((2, BLOCKS)),
            dma((PIECES,)),
            dma((PIECES,)),
            dma((3, 2, BLOCKS)),
            dma((3, 2, BLOCKS)),
            dma((3, THIRDS, BLOCKS)),
            dma((3, 2, THIRDS, BLOCKS)),
            dma((3, RINGS, BLOCKS)),
            dma((3, RINGS, BLOCKS)),
            dma((BLOCKS,)),
            dma((BLOCKS,)),
            dma((BLOCKS,)),
            dma((3,)),
            dma((2, MARGIN // 256)),
            dma((2, MARGIN // 256)),
            dma((GROUP,)),
            dma((GROUP,)),
            dma((GROUP,)),
            dma((GROUP,)),
            dma((GROUP,)),
            dma((GROUP,)),
        ],
        compiler_params=pltpu.CompilerParams(
            collective_id=0, has_side_effects=True, vmem_limit_bytes=64 * 1024 * 1024 - 256 * 1024
        ),
    )(residual, lower_factor, upper_factor, margin_rows, blend)


def scale_kernel(blended, scale, gram_in, basis, gram):
    factor = scale[:, 0:1]
    basis[0] = (blended[...].astype(jnp.float32) * factor).astype(jnp.bfloat16)
    gram[...] = gram_in[...].astype(jnp.float32)


def scaled(blended, scale, gram):
    rows = 256

    def block(width):
        return pl.BlockSpec((rows, width), lambda i: (i, 0))

    return pl.pallas_call(
        scale_kernel,
        grid=(SHOTS // rows,),
        out_shape=(
            jax.ShapeDtypeStruct((1, SHOTS, UNKNOWNS), jnp.bfloat16),
            jax.ShapeDtypeStruct((SHOTS, SHOTS), jnp.float32),
        ),
        in_specs=[block(UNKNOWNS), block(128), block(SHOTS)],
        out_specs=(pl.BlockSpec((1, rows, UNKNOWNS), lambda i: (0, i, 0)), block(SHOTS)),
    )(blended, scale, gram)


def body(residual, lower_factor, upper_factor, margin_rows, blend):
    blended, scale, gram = apply(residual, lower_factor, upper_factor, margin_rows, blend)
    return scaled(blended, scale, gram)


def solution(mesh):
    return jax.shard_map(
        body,
        mesh=mesh,
        in_specs=(
            P("sub", "blk", None),
            P("sub", "blk", None),
            P("sub", "blk", None),
            P("sub", None, None),
            P("sub", None, None),
        ),
        out_specs=(P("sub", "blk", None), P("blk", None)),
        check_vma=False,
    )
```

```python
import functools

import jax
import jax.numpy as jnp
from jax import lax
from jax.experimental import pallas as pl
from jax.experimental.pallas import tpu as pltpu
from jax.sharding import PartitionSpec as P

MESH = pl.DeviceIdType.MESH
UNKNOWNS = 3072
SHOTS = 512
BLOCK = 384
THIRDS = 3
PICKED = UNKNOWNS // 16
THIRD = BLOCK // THIRDS
BLOCKS = UNKNOWNS // BLOCK
RINGS = 4
PIECES = 4
PIECE = SHOTS // PIECES
MARGIN = 512
GROUP = 16
SHARE = SHOTS // GROUP


def times_rows(left, right):
    return lax.dot_general(
        left, right, (((1,), (1,)), ((), ())), preferred_element_type=jnp.float32
    )


def columns(k):
    return pl.ds(pl.multiple_of(k * BLOCK, BLOCK), BLOCK)


def apply_kernel(
    cells,
    rhs_in,
    lower_in,
    upper_in,
    rows_in,
    blend_in,
    blended_out,
    scale_out,
    gram_out,
    rhs,
    lower,
    upper,
    interim,
    local,
    final,
    picks,
    at,
    fresh,
    neighbour,
    rhs_at,
    raw,
    outgoing,
    incoming,
    reduced,
    scale,
    mask,
    squares,
    own_sem,
    x_recv,
    x_send,
    r_recv,
    r_send,
    near_recv,
    near_send,
    far_recv,
    far_send,
    sib_recv,
    sib_send,
    ret_recv,
    ret_send,
    out_sem,
    store_sem,
    side_send,
    side_recv,
    sq_send,
    sq_recv,
    raw_send,
    raw_recv,
    gram_send,
    gram_recv,
):
    sub = lax.axis_index("sub")
    blk = lax.axis_index("blk")
    core = sub % 2
    pair = sub - core
    half = blk // RINGS
    y = blk % RINGS
    guest = core != half
    home = core == half
    partner = (pair + 1 - core, (1 - half) * RINGS + y)
    sibling = (pair + 1 - core, blk)
    up = (sub, half * RINGS + (y + 1) % RINGS)
    down = (sub, half * RINGS + (y + 3) % RINGS)
    opposite = (sub, (1 - half) * RINGS + y)

    def mate(d):
        return ((sub + d) % GROUP, blk)

    def each_mate(step):
        def go(d, carry):
            step(d)
            return carry

        lax.fori_loop(1, GROUP, go, 0)

    barrier = pltpu.get_barrier_semaphore()
    for other in (partner, opposite, up, down):
        pl.semaphore_signal(barrier, inc=1, device_id=other, device_id_type=MESH)
    each_mate(
        lambda d: pl.semaphore_signal(barrier, inc=1, device_id=mate(d), device_id_type=MESH)
    )
    pl.semaphore_wait(barrier, 4 + GROUP - 1)

    sources = (lower_in, upper_in)
    holds = (lower, upper)
    factor = (0, 1, 1)
    ring = (core, half, 1 - half)

    def block(v, offset):
        return ring[v] * RINGS + (y + offset) % RINGS

    def span(w, b):
        return (0, b + 1) if w == 0 else (b, BLOCKS)

    def remote(src, dst, send, recv, device):
        return pltpu.make_async_remote_copy(
            src_ref=src,
            dst_ref=dst,
            send_sem=send,
            recv_sem=recv,
            device_id=device,
            device_id_type=MESH,
        )

    def whole(v, b, k):
        return holds[factor[v]].at[b, :, columns(k)]

    def part(v, b, k, p):
        return holds[factor[v]].at[b, pl.ds(p * THIRD, THIRD), columns(k)]

    def rising(v, target):
        if factor[v] == 0:
            return jnp.where(target == 2, 3, jnp.where(target == 1, 2, 1))
        return jnp.where(target == 1, 0, jnp.where(target == 2, 1, 2))

    def exchange(w, k):
        return remote(
            sources[w].at[0, :, columns(k)],
            whole(w, blk, k),
            x_send.at[w, k],
            x_recv.at[w, k],
            partner if w == 0 else opposite,
        )

    def exchange_rhs(i):
        rows = pl.ds(i * PIECE, PIECE)
        return remote(rhs_in.at[0, rows], rhs.at[rows], r_send.at[i], r_recv.at[i], partner)

    def to_near(v, k, upward, src):
        d = 0 if upward else 1
        return remote(
            src,
            whole(v, block(v, 0), k),
            near_send.at[v, d, k],
            near_recv.at[v, d, k],
            up if upward else down,
        )

    def to_far(v, b, k, p, upward):
        return remote(
            part(v, b, k, p),
            part(v, b, k, p),
            far_send.at[v, 0 if upward else 1, p, k],
            far_recv.at[v, p, k],
            up if upward else down,
        )

    def each_far(v, upward, step):
        target = (y + (1 if upward else 3)) % RINGS
        for p in range(THIRDS):

            @pl.when((p < rising(v, target)) if upward else (p >= rising(v, target)))
            def _():
                step(p)

    def to_sibling(v, b, slot, k, src):
        return remote(
            src,
            whole(v, b, k),
            sib_send.at[v, slot, k],
            sib_recv.at[v, slot, k],
            sibling,
        )

    def each(v, b, step):
        first, last = span(factor[v], b)

        def go(k, carry):
            step(k)
            return carry

        lax.fori_loop(first, last, go, 0)

    def send_own(v, k, src):
        to_near(v, k, True, src).start()
        to_near(v, k, False, src).start()
        to_sibling(v, block(v, 0), 0, k, src).start()

    def own_from_input(v):
        each(
            v,
            block(v, 0),
            lambda k: send_own(v, k, sources[factor[v]].at[0, :, columns(k)]),
        )

    def own_from_partner(v):
        def step(k):
            here = whole(v, block(v, 0), k)
            w = factor[v]
            remote(here, here, x_send.at[w, k], x_recv.at[w, k], partner).wait_recv()
            send_own(v, k, here)

        each(v, block(v, 0), step)

    def relay_from(v, upward, k):
        d = 0 if upward else 1
        b = block(v, 3 if upward else 1)
        here = whole(v, b, k)
        remote(
            here, here, near_send.at[v, d, k], near_recv.at[v, d, k], up if upward else down
        ).wait_recv()
        each_far(v, upward, lambda p: to_far(v, b, k, p, upward).start())
        to_sibling(v, b, 1 + d, k, here).start()

    def pick(i):
        place = pl.ds(pl.multiple_of(i * PICKED, PICKED), PICKED)
        unknown = lax.broadcasted_iota(jnp.int32, (PICKED, MARGIN), 0) + i * PICKED
        for side in range(2):
            hit = unknown == rows_in[0, side : side + 1, :]
            picks[place, side * MARGIN : (side + 1) * MARGIN] = jnp.where(
                hit, jnp.float32(1), jnp.float32(0)
            ).astype(jnp.bfloat16)

    def relay_near(v):
        def go(j, carry):
            if v == 0:
                pick(2 * j)
                pick(2 * j + 1)
            for upward in (True, False):
                first, last = span(factor[v], block(v, 3 if upward else 1))

                @pl.when(first + j < last)
                def _():
                    relay_from(v, upward, first + j)

            return carry

        lax.fori_loop(0, BLOCKS, go, 0)

    def relay_across(v):
        b = block(v, 2)

        def step(k):
            for p in range(THIRDS):
                to_far(v, b, k, p, True).wait_recv()
            to_sibling(v, b, 3, k, whole(v, b, k)).start()

        each(v, b, step)

    def own_copy(w):
        return pltpu.make_async_copy(sources[w].at[0], holds[w].at[blk], own_sem.at[w])

    def rhs_copy():
        return pltpu.make_async_copy(rhs_in.at[0], rhs, own_sem.at[2])

    def turn(t):
        return jnp.where(t == 0, 0, jnp.where(t == 1, 3, t - 1))

    def from_sibling(v, b, slot):
        each(v, b, lambda k: to_sibling(v, b, slot, k, whole(v, b, k)).wait_recv())

    def lower_from_sibling(slot):
        from_sibling(0, (1 - core) * RINGS + (y + turn(slot)) % RINGS, slot)

    @pl.when(home)
    def _():
        own_from_input(0)
        rhs_copy().start()
        own_copy(0).start()
        own_copy(1).start()

    @pl.when(guest)
    def _():
        each(0, blk, lambda k: exchange(0, k).start())

        @pl.when(half == 0)
        def _():
            each(1, blk, lambda k: exchange(1, k).start())

    @pl.when(home)
    def _():
        relay_near(0)
        lower_from_sibling(0)

        @pl.when(y != 1)
        def _():
            own_from_input(1)

        relay_across(0)
        lower_from_sibling(1)
        lower_from_sibling(2)

        @pl.when(y == 1)
        def _():
            own_from_input(1)

        own_from_partner(2)
        relay_near(1)
        rhs_copy().wait()
        own_copy(0).wait()
        own_copy(1).wait()

    @pl.when(guest)
    def _():
        own_from_partner(0)
        for i in range(PIECES):
            exchange_rhs(i).start()

        @pl.when(half == 1)
        def _():
            each(1, blk, lambda k: exchange(1, k).start())

        relay_near(0)
        relay_across(0)
        for i in range(PIECES):
            exchange_rhs(i).wait_recv()
        lower_from_sibling(0)
        lower_from_sibling(1)
        lower_from_sibling(2)

    lower_from_sibling(3)

    for b in range(BLOCKS):
        stop = (b + 1) * BLOCK
        interim[:, b * BLOCK : stop] = (
            times_rows(lower[b, :, :stop], rhs[:, :stop]).astype(jnp.bfloat16).T
        )

    @pl.when(guest)
    def _():
        rhs_copy().start()

    @pl.when(home)
    def _():
        relay_near(2)
        relay_across(1)

    def back(b):
        return remote(
            local.at[:, columns(b)],
            final.at[:, columns(b)],
            ret_send.at[b],
            ret_recv.at[b],
            partner,
        )

    def keep(b):
        return pltpu.make_async_copy(
            local.at[:, columns(b)], final.at[:, columns(b)], out_sem.at[b]
        )

    def solve_step(t, carry):
        first_half = (t == 0) | (t == 2) | (t == 3) | (t == 6)
        slot = jnp.where(t < 2, 0, jnp.where(t > 5, 3, 1 + t % 2))
        this = jnp.where(first_half, half, 1 - half) * RINGS + (y + turn(slot)) % RINGS

        @pl.when(home & (t == 6))
        def _():
            relay_across(2)

        @pl.when(guest & first_half)
        def _():
            from_sibling(1, this, slot)

        @pl.when(guest & jnp.logical_not(first_half))
        def _():
            from_sibling(2, this, slot)

        for b in range(BLOCKS):

            @pl.when(this == b)
            def _():
                start = b * BLOCK
                local[:, start : start + BLOCK] = (
                    times_rows(upper[b, :, start:], interim[:, start:]).astype(jnp.bfloat16).T
                )

        @pl.when(guest)
        def _():
            back(this).start()

        @pl.when(home)
        def _():
            keep(this).start()

        return carry

    lax.fori_loop(0, BLOCKS, solve_step, 0)

    @pl.when(guest)
    def _():
        rhs_copy().wait()

    def picked(values):
        return lambda lanes: jnp.dot(
            values[...], picks[:, lanes], preferred_element_type=jnp.float32
        ).astype(jnp.bfloat16)

    mask[...] = times_rows(jnp.ones((16, 2 * MARGIN), jnp.bfloat16), picks[...])
    at_rhs = picked(rhs)
    for lanes in range(0, 2 * MARGIN, 256):
        rhs_at[:, lanes : lanes + 256] = at_rhs(slice(lanes, lanes + 256))

    def sent(v):
        def own_sent(k):
            here = whole(v, block(v, 0), k)
            to_near(v, k, True, here).wait_send()
            to_near(v, k, False, here).wait_send()
            to_sibling(v, block(v, 0), 0, k, here).wait_send()

        each(v, block(v, 0), own_sent)
        for upward in (True, False):
            b = block(v, 3 if upward else 1)

            def near_sent(k):
                each_far(v, upward, lambda p: to_far(v, b, k, p, upward).wait_send())
                to_sibling(v, b, 1 if upward else 2, k, whole(v, b, k)).wait_send()

            each(v, b, near_sent)
        b = block(v, 2)
        each(v, b, lambda k: to_sibling(v, b, 3, k, whole(v, b, k)).wait_send())

    sent(0)

    @pl.when(home)
    def _():
        sent(1)
        sent(2)

    @pl.when(guest)
    def _():
        for w in range(2):
            each(w, blk, lambda k: exchange(w, k).wait_send())
        for i in range(PIECES):
            exchange_rhs(i).wait_send()

    def finish(b, carry):
        @pl.when(guest)
        def _():
            back(b).wait()

        @pl.when(home)
        def _():
            keep(b).wait()

        return carry

    lax.fori_loop(0, BLOCKS, finish, 0)

    def side_copy(side, i):
        lanes = pl.ds(i * 256, 256)
        return remote(
            at.at[side, :, lanes],
            neighbour.at[1 - side, :, lanes],
            side_send.at[side, i],
            side_recv.at[1 - side, i],
            ((sub + (GROUP - 1 if side == 0 else 1)) % GROUP, blk),
        )

    lasting = (sub > 0, sub < GROUP - 1)

    at_side = picked(final)
    for i in range(MARGIN // 256):
        for side in range(2):
            lanes = side * MARGIN + i * 256
            at[side, :, i * 256 : (i + 1) * 256] = at_side(slice(lanes, lanes + 256))

            @pl.when(lasting[side])
            def _():
                side_copy(side, i).start()

    def keep_rows(i, carry):
        place = pl.ds(pl.multiple_of(i * 64, 64), 64)
        rest = jnp.where(mask[0:1, :] > 0.5, 0.0, final[place, :].astype(jnp.float32))
        interim[place, :] = rest.astype(jnp.bfloat16)
        total = jnp.zeros((64, 128), jnp.float32)
        for lane in range(0, UNKNOWNS, 128):
            piece = rest[:, lane : lane + 128]
            total += piece * piece
        scale[place, :] = total
        return carry

    lax.fori_loop(0, SHOTS // 64, keep_rows, 0)
    for lanes in range(0, SHOTS, 256):
        raw[:, lanes : lanes + 256] = times_rows(interim[...], rhs[lanes : lanes + 256, :])

    for side in range(2):
        lanes = slice(side * MARGIN, (side + 1) * MARGIN)

        @pl.when(lasting[side])
        def _():
            for i in range(MARGIN // 256):
                side_copy(1 - side, i).wait_recv()
            value = at[side].astype(jnp.float32)
            other = neighbour[side].astype(jnp.float32)
            fresh[:, lanes] = (
                value + blend_in[0, side : side + 1, :] * (other - value)
            ).astype(jnp.bfloat16)

        @pl.when(jnp.logical_not(lasting[side]))
        def _():
            fresh[:, lanes] = at[side]

    total = scale[...]
    for lane in range(0, 2 * MARGIN, 128):
        piece = fresh[:, lane : lane + 128].astype(jnp.float32)
        total += piece * piece
    across = jnp.sum(total.T, axis=0, keepdims=True)
    squares[0] = jnp.zeros((8, 128), jnp.float32)
    for i in range(SHOTS // 128):
        squares[0, i : i + 1, :] = across[:, i * 128 : (i + 1) * 128]

    def sq_copy(d):
        return remote(squares.at[0], squares.at[d], sq_send.at[d], sq_recv.at[d], mate(d))

    each_mate(lambda d: sq_copy(d).start())

    outgoing[...] = (raw[...] + times_rows(fresh[...], rhs_at[...])).astype(jnp.bfloat16)

    def own_rows(who):
        return pl.ds(pl.multiple_of(who * SHARE, SHARE), SHARE)

    def raw_copy(d):
        return remote(
            outgoing.at[own_rows((sub + d) % GROUP)],
            incoming.at[d],
            raw_send.at[d],
            raw_recv.at[d],
            mate(d),
        )

    each_mate(lambda d: raw_copy(d).start())

    for lane in range(0, UNKNOWNS, BLOCK):
        lanes = slice(lane, lane + BLOCK)
        placed = times_rows(fresh[...], picks[lanes, :])
        local[:, lanes] = jnp.where(
            mask[0:1, lanes] > 0.5, placed, final[:, lanes].astype(jnp.float32)
        ).astype(jnp.bfloat16)
    store_blended = pltpu.make_async_copy(local, blended_out, store_sem.at[0])
    store_blended.start()

    each_mate(lambda d: sq_copy(d).wait_recv())
    grand = squares[0]
    for d in range(1, GROUP):
        grand += squares[d]
    factor = 1.0 / jnp.sqrt(grand / cells + 1e-05)
    for i in range(SHOTS // 128):
        scale[i * 128 : (i + 1) * 128, :] = jnp.broadcast_to(factor[i : i + 1, :], (128, 128)).T
    store_scale = pltpu.make_async_copy(scale, scale_out, store_sem.at[1])
    store_scale.start()

    each_mate(lambda d: raw_copy(d).wait_recv())
    sum_rows = outgoing[own_rows(sub), :].astype(jnp.float32)
    for d in range(1, GROUP):
        sum_rows += incoming[d].astype(jnp.float32)
    reduced[...] = (sum_rows * (scale[own_rows(sub), 0:1] / cells)).astype(jnp.bfloat16)

    def gram_copy(d):
        return remote(
            reduced,
            gram_out.at[own_rows(sub)],
            gram_send.at[d],
            gram_recv.at[d],
            mate(d),
        )

    def gram_sibling():
        return remote(
            reduced, gram_out.at[own_rows(sub)], gram_send.at[0], gram_recv.at[0], sibling
        )

    def gram_forward(d):
        here = gram_out.at[own_rows((sub + GROUP - d) % GROUP)]
        return remote(here, here, gram_send.at[d + 1], gram_recv.at[d + 1], sibling)

    def each_even(step):
        def go(i, carry):
            step(2 * i)
            return carry

        lax.fori_loop(1, GROUP // 2, go, 0)

    store_gram = pltpu.make_async_copy(reduced, gram_out.at[own_rows(sub)], store_sem.at[2])
    store_gram.start()
    each_even(lambda d: gram_copy(d).start())
    gram_sibling().start()

    def forward(d):
        gram_copy(d).wait_recv()
        gram_forward(d).start()

    each_even(forward)
    gram_sibling().wait_recv()
    each_even(lambda d: gram_forward(d).wait_recv())
    for side in range(2):

        @pl.when(lasting[side])
        def _():
            for i in range(MARGIN // 256):
                side_copy(side, i).wait_send()

    each_mate(lambda d: sq_copy(d).wait_send())
    each_mate(lambda d: raw_copy(d).wait_send())
    each_even(lambda d: gram_copy(d).wait_send())
    gram_sibling().wait_send()
    each_even(lambda d: gram_forward(d).wait_send())
    store_blended.wait()
    store_scale.wait()
    store_gram.wait()


def apply(residual, lower_factor, upper_factor, margin_rows, blend):
    dma = pltpu.SemaphoreType.DMA
    hbm = pl.BlockSpec(memory_space=pl.ANY)
    vmem = pl.BlockSpec(memory_space=pltpu.VMEM)
    bf16 = jnp.bfloat16
    return pl.pallas_call(
        functools.partial(apply_kernel, float(GROUP * UNKNOWNS)),
        out_shape=(
            jax.ShapeDtypeStruct((SHOTS, UNKNOWNS), bf16),
            jax.ShapeDtypeStruct((SHOTS, 128), jnp.float32),
            jax.ShapeDtypeStruct((SHOTS, SHOTS), bf16),
        ),
        in_specs=[hbm, hbm, hbm, vmem, vmem],
        out_specs=(hbm, hbm, hbm),
        scratch_shapes=[
            pltpu.VMEM((SHOTS, UNKNOWNS), bf16),
            pltpu.VMEM((BLOCKS, BLOCK, UNKNOWNS), bf16),
            pltpu.VMEM((BLOCKS, BLOCK, UNKNOWNS), bf16),
            pltpu.VMEM((SHOTS, UNKNOWNS), bf16),
            pltpu.VMEM((SHOTS, UNKNOWNS), bf16),
            pltpu.VMEM((SHOTS, UNKNOWNS), bf16),
            pltpu.VMEM((UNKNOWNS, 2 * MARGIN), bf16),
            pltpu.VMEM((2, SHOTS, MARGIN), bf16),
            pltpu.VMEM((SHOTS, 2 * MARGIN), bf16),
            pltpu.VMEM((2, SHOTS, MARGIN), bf16),
            pltpu.VMEM((SHOTS, 2 * MARGIN), bf16),
            pltpu.VMEM((SHOTS, SHOTS), jnp.float32),
            pltpu.VMEM((SHOTS, SHOTS), bf16),
            pltpu.VMEM((GROUP, SHARE, SHOTS), bf16),
            pltpu.VMEM((SHARE, SHOTS), bf16),
            pltpu.VMEM((SHOTS, 128), jnp.float32),
            pltpu.VMEM((16, UNKNOWNS), jnp.float32),
            pltpu.VMEM((GROUP, 8, 128), jnp.float32),
            dma((3,)),
            dma((2, BLOCKS)),
            dma((2, BLOCKS)),
            dma((PIECES,)),
            dma((PIECES,)),
            dma((3, 2, BLOCKS)),
            dma((3, 2, BLOCKS)),
            dma((3, THIRDS, BLOCKS)),
            dma((3, 2, THIRDS, BLOCKS)),
            dma((3, RINGS, BLOCKS)),
            dma((3, RINGS, BLOCKS)),
            dma((BLOCKS,)),
            dma((BLOCKS,)),
            dma((BLOCKS,)),
            dma((3,)),
            dma((2, MARGIN // 256)),
            dma((2, MARGIN // 256)),
            dma((GROUP,)),
            dma((GROUP,)),
            dma((GROUP,)),
            dma((GROUP,)),
            dma((GROUP,)),
            dma((GROUP,)),
        ],
        compiler_params=pltpu.CompilerParams(
            collective_id=0, has_side_effects=True, vmem_limit_bytes=64 * 1024 * 1024 - 256 * 1024
        ),
    )(residual, lower_factor, upper_factor, margin_rows, blend)


def scale_kernel(blended, scale, gram_in, basis, gram):
    factor = scale[:, 0:1]
    basis[0] = (blended[...].astype(jnp.float32) * factor).astype(jnp.bfloat16)
    gram[...] = gram_in[...].astype(jnp.float32)


def scaled(blended, scale, gram):
    rows = 256

    def block(width):
        return pl.BlockSpec((rows, width), lambda i: (i, 0))

    return pl.pallas_call(
        scale_kernel,
        grid=(SHOTS // rows,),
        out_shape=(
            jax.ShapeDtypeStruct((1, SHOTS, UNKNOWNS), jnp.bfloat16),
            jax.ShapeDtypeStruct((SHOTS, SHOTS), jnp.float32),
        ),
        in_specs=[block(UNKNOWNS), block(128), block(SHOTS)],
        out_specs=(pl.BlockSpec((1, rows, UNKNOWNS), lambda i: (0, i, 0)), block(SHOTS)),
    )(blended, scale, gram)


def body(residual, lower_factor, upper_factor, margin_rows, blend):
    blended, scale, gram = apply(residual, lower_factor, upper_factor, margin_rows, blend)
    return scaled(blended, scale, gram)


def solution(mesh):
    return jax.shard_map(
        body,
        mesh=mesh,
        in_specs=(
            P("sub", "blk", None),
            P("sub", "blk", None),
            P("sub", "blk", None),
            P("sub", None, None),
            P("sub", None, None),
        ),
        out_specs=(P("sub", "blk", None), P("blk", None)),
        check_vma=False,
    )
```
